512 devices in a mesh: fft: 32 (over y, x_hi, core), plane: 16 (over z, x_lo).
Axes of the slice: x: 4 (x_hi: 2, x_lo: 2; x = x_hi * 2 + x_lo), y: 8, z: 8, core: 2. Of those that a mesh axis runs over, the one named last changes fastest.
Arguments:
- error_field: float32 [2048, 16, 2048], P('fft', 'plane'), may hold values from -1 to 1
- x_shape: float32 [2048], replicated, may hold values from 0.25 to 1
- y_shape: float32 [2048], replicated, may hold values from 0.25 to 1
Outputs:
- corrected: float32 [2048, 16, 2048], P('fft', 'plane')
The draws below stay inside these ranges and needn't reach their ends.
All inputs are finite; a program needn't handle non-finite values.
Results may differ from the reference program's by a relative error of at most 0.00012.
Values sent between devices are 32-bit elements; how exact they have to be, the bound alone decides.
A program may use at most 64 MiB of HBM per device.

```python
import math
import jax
import jax.numpy as jnp
from jax import lax

N = 2048
PLANES = 16


def levels(rng, dims, shards, low, top_value):
    level = 1.0
    for position, parts in shards:
        steps = jax.random.uniform(jax.random.fold_in(jax.random.fold_in(rng, 6), position), (parts,), jnp.float32, low / len(shards), top_value / len(shards))
        level = level * jnp.repeat(jnp.exp(steps), dims[position] // parts).reshape((-1,) + (1,) * (len(dims) - 1 - position))
    return level


def setup_inputs(seed: int = 0) -> dict:
    key_of = jax.random.split(jax.random.key(seed), 4)
    return {
        "error_field": jnp.clip(jax.random.uniform(key_of[0], (N, PLANES, N), jnp.float32, -1.0, 1.0) * levels(key_of[0], (N, PLANES, N), ((0, 32), (1, 16)), -0.4, 0.0), -1.0, 1.0),
        "x_shape": jnp.clip(jnp.exp(jax.random.uniform(key_of[1], (N,), jnp.float32, math.log(0.25), math.log(1.0))), 0.25, 1.0),
        "y_shape": jnp.clip(jnp.exp(jax.random.uniform(key_of[2], (N,), jnp.float32, math.log(0.25), math.log(1.0))), 0.25, 1.0),
    }


def flipped(values, directions):
    return jnp.roll(jnp.flip(values, directions), 1, directions)

def reference(error_field, x_shape, y_shape):
    field_yzx = jnp.transpose(error_field, (2, 1, 0))
    planes = field_yzx.shape[1]

    def plane_spectrum(plane_index):
        plane_data = lax.dynamic_index_in_dim(field_yzx, plane_index, 1, False)
        return jnp.fft.fft2(plane_data)

    def accumulate(summed, plane_index):
        spectrum = plane_spectrum(plane_index)
        return (summed + (spectrum.real * spectrum.real + spectrum.imag * spectrum.imag), None)
    summed, unused = lax.scan(accumulate, jnp.zeros((N, N), jnp.float32), jnp.arange(planes))
    mean_power = summed / planes
    spectral_bound = y_shape[:, None] * x_shape[None, :] * jnp.sqrt(mean_power)

    def correct(plane_index):
        spectrum = plane_spectrum(plane_index)
        clipped = jnp.clip(spectrum.real, -spectral_bound, spectral_bound) + 1j * jnp.clip(spectrum.imag, -spectral_bound, spectral_bound)
        symmetric = 0.5 * (clipped + jnp.conj(flipped(clipped, (0, 1))))
        spatial = jnp.fft.ifft2(symmetric).real
        return jnp.clip(spatial, -1.0, 1.0)
    corrected = lax.map(correct, jnp.arange(planes))
    return jnp.transpose(corrected, (2, 0, 1))
```

```python
import math

import jax
import jax.numpy as jnp
import ml_dtypes
import numpy as np
from jax import lax
from jax.experimental import pallas as pl
from jax.experimental.pallas import tpu as pltpu
from jax.sharding import PartitionSpec as P

F32 = jnp.float32
BF16 = jnp.bfloat16
N = 2048
FFT = 32
PLANES = 16
OWN = N // FFT
HALF = 64
LANES = 128
CHUNKS = 2
MESH = pl.DeviceIdType.MESH


def two_parts(table):
    table = np.asarray(table, np.float64)
    high = table.astype(np.float32).astype(ml_dtypes.bfloat16)
    low = (table - high.astype(np.float64)).astype(np.float32).astype(ml_dtypes.bfloat16)
    return np.stack([high, low])


def row_order():
    chunk, block, part, step = np.meshgrid(np.arange(2), np.arange(4), np.arange(2), np.arange(8), indexing="ij")
    return part.reshape(-1), (block * 16 + chunk * 8 + step).reshape(-1)


def y_forward_table():
    part, row = row_order()
    angle = 2 * np.pi / LANES * (row[:, None] * np.arange(LANES)[None, :] % LANES)
    cosine, sine = np.cos(angle), np.sin(angle)
    part = part[:, None]
    table = np.concatenate([np.where(part == 0, cosine, -sine), np.where(part == 0, sine, cosine)], 1)
    extra = np.zeros((16, 2 * LANES))
    extra[0, :LANES] = 1 - 2 * (np.arange(LANES) % 2)
    return two_parts(np.concatenate([table, extra], 0))


def y_inverse_table():
    part, row = row_order()
    column = np.arange(LANES)
    angle = 2 * np.pi / LANES * (row[:, None] * column[None, :] % LANES)
    cosine, sine = np.cos(angle), np.sin(angle)
    part, row = part[:, None], row[:, None]
    plain = np.concatenate([np.where(part == 0, cosine, -sine), np.where(part == 0, sine, cosine)], 1)
    sign = (1 - 2 * (column % 2))[None, :]
    first = np.where(part == 0, np.where(row == 0, 1.0, 2 * cosine), np.where(row == 0, sign, -2 * sine))
    return two_parts(np.concatenate([plain, first], 1) / (N * N))


def x_table(direction):
    line = np.arange(HALF)
    angle = 2 * np.pi / HALF * (line[:, None] * line[None, :] % HALF)
    both = np.eye(2)
    cosine, sine = np.kron(both, np.cos(angle)), direction * np.kron(both, np.sin(angle))
    return two_parts(np.block([[cosine, sine], [-sine, cosine]]))


def y_twist():
    angle = 2 * np.pi / N * (np.arange(16)[:, None] * np.arange(LANES)[None, :] % N)
    return np.stack([np.cos(angle), np.sin(angle)]).astype(np.float32)


def x_twist():
    column = np.arange(LANES) % HALF
    angle = 2 * np.pi / N * (np.arange(FFT)[:, None] * column[None, :] % N)
    table = np.stack([np.cos(angle), np.sin(angle)]).astype(np.float32)
    return np.broadcast_to(table[:, :, None, :], (2, FFT, 8, LANES)).copy()


def split(values):
    high = values.astype(BF16)
    return high, (values - high.astype(F32)).astype(BF16)


def dot(left, right, dims):
    return lax.dot_general(left, right, (dims, ((), ())), preferred_element_type=F32)


def product(left, right, dims):
    (left_high, left_low), (right_high, right_low) = left, right
    return dot(left_high, right_high, dims) + (dot(left_low, right_high, dims) + dot(left_high, right_low, dims))


def turn(value, part, whole, direction):
    real, imag = value
    part = part % whole
    eighth = 8 * part
    if eighth % whole == 0:
        eighth = eighth // whole
        root = math.sqrt(0.5)
        if eighth == 0:
            return value
        if eighth == 4:
            return (-real, -imag)
        if eighth == 2 or eighth == 6:
            return (-imag, real) if (eighth == 2) == (direction > 0) else (imag, -real)
    cosine, sine = math.cos(2 * math.pi * part / whole), direction * math.sin(2 * math.pi * part / whole)
    return (real * cosine - imag * sine, real * sine + imag * cosine)


def plus(left, right):
    return (left[0] + right[0], left[1] + right[1])


def minus(left, right):
    return (left[0] - right[0], left[1] - right[1])


def small_dft(values, direction):
    size = len(values)
    if size == 1:
        return values
    even = small_dft(values[0::2], direction)
    odd = small_dft(values[1::2], direction)
    odd = [turn(odd[index], index, size, direction) for index in range(size // 2)]
    return [plus(even[index], odd[index]) for index in range(size // 2)] + [
        minus(even[index], odd[index]) for index in range(size // 2)
    ]


def dft32(real, imag, direction):
    shape = (4, 8) + real.shape[1:]
    real, imag = real.reshape(shape), imag.reshape(shape)
    first = small_dft([(real[u], imag[u]) for u in range(4)], direction)
    second = []
    for v in range(8):
        turned = [turn((first[w][0][v], first[w][1][v]), w * v, 32, direction) for w in range(4)]
        second.append((jnp.stack([value[0] for value in turned]), jnp.stack([value[1] for value in turned])))
    done = small_dft(second, direction)
    flat = (32,) + real.shape[2:]
    return (
        jnp.stack([value[0] for value in done]).reshape(flat),
        jnp.stack([value[1] for value in done]).reshape(flat),
    )


def real_dft(values):
    size = len(values)
    if size == 2:
        return [values[0] + values[1], values[0] - values[1]]
    even, odd = real_dft(values[0::2]), real_dft(values[1::2])
    half, quarter = size // 2, size // 4
    out = [None] * (half + 1)
    out[0], out[half] = even[0] + odd[0], even[0] - odd[0]
    out[quarter] = (even[quarter], -odd[quarter])
    for index in range(1, quarter):
        turned = turn(odd[index], index, size, -1)
        out[index] = plus(even[index], turned)
        back = minus(even[index], turned)
        out[half - index] = (back[0], -back[1])
    return out


def real_inverse(values):
    half = len(values) - 1
    size = 2 * half
    if size == 2:
        return [values[0] + values[1], values[0] - values[1]]
    quarter = size // 4
    even, odd = [None] * (quarter + 1), [None] * (quarter + 1)
    even[0], odd[0] = values[0] + values[half], values[0] - values[half]
    even[quarter], odd[quarter] = 2.0 * values[quarter][0], -2.0 * values[quarter][1]
    for index in range(1, quarter):
        mirror = (values[half - index][0], -values[half - index][1])
        even[index] = plus(values[index], mirror)
        odd[index] = turn(minus(values[index], mirror), index, size, 1)
    out = [None] * size
    out[0::2], out[1::2] = real_inverse(even), real_inverse(odd)
    return out


def y_operands(field, twist_cos, twist_sin):
    parts = real_dft([field[:, LANES * index : LANES * (index + 1)] for index in range(16)])
    sign = 1.0 - 2.0 * (lax.broadcasted_iota(jnp.int32, (OWN, LANES), 1) % 2).astype(F32)

    def twisted(index):
        cosine, sine = twist_cos[index][None, :], twist_sin[index][None, :]
        if index == 8:
            return jnp.concatenate([parts[8] * cosine, -parts[8] * sine], 1)
        real, imag = parts[index]
        return jnp.concatenate([real * cosine + imag * sine, imag * cosine - real * sine], 1)

    signs = jnp.concatenate([sign, sign], 1)
    out = [jnp.concatenate([jnp.concatenate([parts[0], jnp.zeros_like(parts[0])], 1), twisted(8)], 0)]
    for index in range(1, 8):
        value = twisted(index)
        out.append(jnp.concatenate([value, value * signs], 0))
    return out


def y_result(sums, twist_cos, twist_sin):
    sign = 1.0 - 2.0 * (lax.broadcasted_iota(jnp.int32, (OWN, LANES), 1) % 2).astype(F32)
    values = [sums[0][:OWN, 2 * LANES :]]
    for index in range(1, 8):
        real = sums[index][:OWN, :LANES] + sign * sums[index][OWN:, :LANES]
        imag = sums[index][:OWN, LANES:] + sign * sums[index][OWN:, LANES:]
        cosine, sine = twist_cos[index][None, :], twist_sin[index][None, :]
        values.append((real * cosine - imag * sine, real * sine + imag * cosine))
    real, imag = sums[0][OWN:, :LANES], sums[0][OWN:, LANES : 2 * LANES]
    values.append(2.0 * (real * twist_cos[8][None, :] - imag * twist_sin[8][None, :]))
    return jnp.concatenate([jnp.clip(value, -1.0, 1.0) for value in real_inverse(values)], 1)


def x_forward(real, imag, table, twist_cos, twist_sin):
    real, imag = dft32(real, imag, -1)
    both = jnp.concatenate([real * twist_cos + imag * twist_sin, imag * twist_cos - real * twist_sin], 2)
    out = product(split(both.reshape(256, 256)), table, ((1,), (0,)))
    return out.reshape(FFT, 8, 2 * LANES)


def x_inverse(values, table, twist_cos, twist_sin):
    out = product(split(values.reshape(256, 256)), table, ((1,), (0,))).reshape(FFT, 8, 2 * LANES)
    real, imag = out[:, :, :LANES], out[:, :, LANES:]
    return dft32(real * twist_cos - imag * twist_sin, real * twist_sin + imag * twist_cos, 1)


SEND, RECV, POWER, MEAN, BACK = range(5)


def kernel(
    field_hbm, yf_hbm, yi_hbm, xf_hbm, xi_hbm, yt_hbm, xt_hbm, xs_hbm, y_shape,
    out_hbm,
    field, yf, yi, xf, xi, yt, xt, xs, out,
    sent, received, spec, power, powers, root, bound, back, returned, sym,
    load_sem, send_sem, recv_sem,
):
    me = lax.axis_index("fft")
    plane = lax.axis_index("plane")
    special = me == 0

    barrier = pltpu.get_barrier_semaphore()

    def fft_peer(step):
        return lax.rem(me + step, FFT)

    def plane_peer(step):
        return lax.rem(plane + step, PLANES)

    loads = []
    for index, (source, target) in enumerate(
        [(field_hbm, field), (yf_hbm, yf), (yt_hbm, yt), (xf_hbm, xf), (xt_hbm, xt), (xs_hbm, xs), (xi_hbm, xi), (yi_hbm, yi)]
    ):
        copy = pltpu.make_async_copy(source, target, load_sem.at[index])
        copy.start()
        loads.append(copy)

    @pl.loop(1, FFT)
    def _(step):
        pl.semaphore_signal(barrier, inc=1, device_id=(fft_peer(step), plane), device_id_type=MESH)

    @pl.loop(1, PLANES)
    def _(step):
        pl.semaphore_signal(barrier, inc=1, device_id=(me, plane_peer(step)), device_id_type=MESH)

    for copy in loads[:3]:
        copy.wait()
    operands = [split(value) for value in y_operands(field[:, 0, :], yt[0], yt[1])]
    for index, operand in enumerate(operands):
        done = product((yf[0, :128], yf[1, :128]), operand, ((1,), (1,)))
        if index == 0:
            extra = product((yf[0, 128:], yf[1, 128:]), operand, ((1,), (1,)))[0:1, :]
            row = lax.broadcasted_iota(jnp.int32, (128, LANES), 0)
            lane = lax.broadcasted_iota(jnp.int32, (128, LANES), 1)
            done = jnp.where((row == 8) & (lane < HALF), extra, done)
        sent[:, 4 * index : 4 * index + 4] = done.reshape(2, 4, 16, LANES)
    for chunk in range(CHUNKS):
        received[chunk, me] = sent[chunk, me]

    pl.semaphore_wait(barrier, FFT - 1 + PLANES - 1)

    def all_to_all(source, target, chunk, kind):
        @pl.loop(1, FFT)
        def _(step):
            peer = fft_peer(step)
            pltpu.make_async_remote_copy(
                src_ref=source.at[chunk, peer],
                dst_ref=target.at[chunk, me],
                send_sem=send_sem.at[kind, chunk],
                recv_sem=recv_sem.at[kind, chunk],
                device_id=(peer, plane),
                device_id_type=MESH,
            ).start()

    def to_planes(source, target, chunk, kind):
        @pl.loop(1, PLANES)
        def _(step):
            peer = plane_peer(step)
            pltpu.make_async_remote_copy(
                src_ref=source(peer),
                dst_ref=target,
                send_sem=send_sem.at[kind, chunk],
                recv_sem=recv_sem.at[kind, chunk],
                device_id=(me, peer),
                device_id_type=MESH,
            ).start()

    def wait_for(ref, sem):
        pltpu.make_async_copy(ref, ref, sem).wait()

    all_to_all(sent, received, 0, SEND)
    all_to_all(sent, received, 1, SEND)

    for copy in loads[3:]:
        copy.wait()
    group, block = me // 4, lax.rem(me, 4)
    row = lax.broadcasted_iota(jnp.int32, (8, LANES), 0)
    lane = lax.broadcasted_iota(jnp.int32, (8, LANES), 1)
    for chunk in range(CHUNKS):
        here, other = jnp.zeros((8, LANES), F32), jnp.zeros((8, LANES), F32)
        for half in range(2):
            for step in range(8):
                line = 16 * block + 8 * chunk + step
                ky = jnp.where(group == 0, 8 * half + 16 * line, group + 16 * (line + 64 * half))
                place = (row == step) & (lane // HALF == half)
                here = jnp.where(place, y_shape[ky], here)
                other = jnp.where(place, y_shape[lax.rem(N - ky, N)], other)
        bound[0, chunk] = here[None] * xs[0]
        bound[1, chunk] = other[None] * xs[1]

    @pl.when(special)
    def _():
        here = jnp.where(lane < HALF, y_shape[0], y_shape[N // 2])
        bound[0, 2] = here[None] * xs[0]
        bound[1, 2] = here[None] * xs[1]

    def along_x(real, imag, chunk):
        done = x_forward(real, imag, (xf[0], xf[1]), xt[0], xt[1])
        spec[chunk] = done
        real, imag = done[:, :, :LANES], done[:, :, LANES:]
        power[chunk] = real * real + imag * imag
        mine = pl.ds(2 * plane, 2)
        powers[chunk, plane] = power[chunk, mine]
        to_planes(lambda peer: power.at[chunk, pl.ds(2 * peer, 2)], powers.at[chunk, plane], chunk, POWER)

    def average(chunk):
        wait_for(powers.at[chunk, pl.ds(0, PLANES - 1)], recv_sem.at[POWER, chunk])
        mine = pl.ds(2 * plane, 2)
        total = powers[chunk, 0]
        for index in range(1, PLANES):
            total = total + powers[chunk, index]
        root[chunk, mine] = jnp.sqrt(total * (1.0 / PLANES))
        to_planes(lambda peer: root.at[chunk, mine], root.at[chunk, mine], chunk, MEAN)

    def clipped(chunk):
        wait_for(root.at[chunk, pl.ds(0, 2 * (PLANES - 1))], recv_sem.at[MEAN, chunk])
        here, other = bound[0, chunk] * root[chunk], bound[1, chunk] * root[chunk]
        real, imag = spec[chunk, :, :, :LANES], spec[chunk, :, :, LANES:]
        return [
            0.5 * (jnp.clip(value, -here, here) + jnp.clip(value, -other, other)) for value in (real, imag)
        ]

    def first_half(chunk):
        wait_for(received.at[chunk, pl.ds(0, FFT - 1)], recv_sem.at[SEND, chunk])
        along_x(received[chunk, :, :8], received[chunk, :, 8:], chunk)

    def second_half(chunk):
        real, imag = clipped(chunk)
        sym[:, :, :LANES] = real
        sym[:, :, LANES:] = imag
        if chunk == 0:

            @pl.when(special)
            def _():
                real, imag = clipped(2)
                shape = (FFT, 8, LANES)
                place = (lax.broadcasted_iota(jnp.int32, shape, 1) == 0) & (
                    lax.broadcasted_iota(jnp.int32, shape, 2) < HALF
                )
                sym[:, :, :LANES] = jnp.where(place, real - pltpu.roll(imag, HALF, 2), sym[:, :, :LANES])
                sym[:, :, LANES:] = jnp.where(place, imag + pltpu.roll(real, HALF, 2), sym[:, :, LANES:])

        real, imag = x_inverse(sym[...], (xi[0], xi[1]), xt[0], xt[1])
        back[chunk, :, :8] = real
        back[chunk, :, 8:] = imag
        returned[chunk, me] = back[chunk, me]
        all_to_all(back, returned, chunk, BACK)

    first_half(0)

    @pl.when(special)
    def _():
        real, imag = received[0, :, :8], received[0, :, 8:]
        halves = lax.broadcasted_iota(jnp.int32, real.shape, 2) < HALF
        along_x(jnp.where(halves, real, pltpu.roll(imag, HALF, 2)), jnp.zeros_like(real), 2)

    average(0)

    @pl.when(special)
    def _():
        average(2)

    first_half(1)
    second_half(0)
    average(1)
    second_half(1)

    for chunk in range(CHUNKS):
        wait_for(returned.at[chunk, pl.ds(0, FFT - 1)], recv_sem.at[BACK, chunk])
    sums = []
    for index in range(8):
        rows = jnp.concatenate([returned[chunk, 4 * index : 4 * index + 4].reshape(64, LANES) for chunk in range(CHUNKS)], 0)
        width = 2 * LANES if index else 3 * LANES
        sums.append(product(split(rows), (yi[0, :, :width], yi[1, :, :width]), ((0,), (0,))))
    out[:, 0, :] = y_result(sums, yt[0], yt[1])
    store = pltpu.make_async_copy(out, out_hbm, load_sem.at[0])
    store.start()

    for chunk in range(CHUNKS):
        for kind in (SEND, BACK):
            wait_for(received.at[chunk, pl.ds(0, FFT - 1)], send_sem.at[kind, chunk])
        for kind in (POWER, MEAN):
            wait_for(powers.at[chunk, pl.ds(0, PLANES - 1)], send_sem.at[kind, chunk])

    @pl.when(special)
    def _():
        for kind in (POWER, MEAN):
            wait_for(powers.at[2, pl.ds(0, PLANES - 1)], send_sem.at[kind, 2])

    store.wait()


def correct(error_field, x_shape, y_shape):
    shape = error_field.shape
    factors = jnp.stack([x_shape, jnp.roll(x_shape[::-1], 1)]).reshape(2, HALF, FFT).transpose(0, 2, 1)
    factors = jnp.broadcast_to(factors[:, :, None, None, :], (2, FFT, 8, 2, HALF)).reshape(2, FFT, 8, LANES)
    operands = [
        error_field, y_forward_table(), y_inverse_table(), x_table(-1), x_table(1), y_twist(), x_twist(), factors,
    ]
    operands = [jnp.asarray(operand) for operand in operands]
    anywhere = pl.BlockSpec(memory_space=pl.ANY)
    return pl.pallas_call(
        kernel,
        out_shape=jax.ShapeDtypeStruct(shape, F32),
        in_specs=[anywhere] * 8 + [pl.BlockSpec(memory_space=pltpu.SMEM)],
        out_specs=anywhere,
        scratch_shapes=[pltpu.VMEM(operand.shape, operand.dtype) for operand in operands]
        + [
            pltpu.VMEM(shape, F32),
            pltpu.VMEM((CHUNKS, FFT, 16, LANES), F32),
            pltpu.VMEM((CHUNKS, FFT, 16, LANES), F32),
            pltpu.VMEM((CHUNKS + 1, FFT, 8, 2 * LANES), F32),
            pltpu.VMEM((CHUNKS + 1, FFT, 8, LANES), F32),
            pltpu.VMEM((CHUNKS + 1, PLANES, 2, 8, LANES), F32),
            pltpu.VMEM((CHUNKS + 1, FFT, 8, LANES), F32),
            pltpu.VMEM((2, CHUNKS + 1, FFT, 8, LANES), F32),
            pltpu.VMEM((CHUNKS, FFT, 16, LANES), F32),
            pltpu.VMEM((CHUNKS, FFT, 16, LANES), F32),
            pltpu.VMEM((FFT, 8, 2 * LANES), F32),
            pltpu.SemaphoreType.DMA((8,)),
            pltpu.SemaphoreType.DMA((5, CHUNKS + 1)),
            pltpu.SemaphoreType.DMA((5, CHUNKS + 1)),
        ],
        compiler_params=pltpu.CompilerParams(
            collective_id=0, has_side_effects=True, vmem_limit_bytes=48 * 1024 * 1024
        ),
    )(*operands, y_shape)


def solution(mesh):
    placed = (P("fft", "plane", None), P(), P())
    return jax.shard_map(
        correct, mesh=mesh, in_specs=placed, out_specs=P("fft", "plane", None), check_vma=False
    )
```

```python
import math

import jax
import jax.numpy as jnp
import ml_dtypes
import numpy as np
from jax import lax
from jax.experimental import pallas as pl
from jax.experimental.pallas import tpu as pltpu
from jax.sharding import PartitionSpec as P

F32 = jnp.float32
BF16 = jnp.bfloat16
N = 2048
FFT = 32
PLANES = 16
OWN = N // FFT
HALF = 64
LANES = 128
CHUNKS = 4
SPECIAL = CHUNKS
MESH = pl.DeviceIdType.MESH


def two_parts(table):
    table = np.asarray(table, np.float64)
    high = table.astype(np.float32).astype(ml_dtypes.bfloat16)
    low = (table - high.astype(np.float64)).astype(np.float32).astype(ml_dtypes.bfloat16)
    return np.stack([high, low])


def row_order():
    block, part, step = np.meshgrid(np.arange(16), np.arange(2), np.arange(4), indexing="ij")
    return part.reshape(-1), (block * 4 + step).reshape(-1)


def y_forward_table():
    part, row = row_order()
    angle = 2 * np.pi / LANES * (row[:, None] * np.arange(LANES)[None, :] % LANES)
    cosine, sine = np.cos(angle), np.sin(angle)
    part = part[:, None]
    table = np.concatenate([np.where(part == 0, cosine, -sine), np.where(part == 0, sine, cosine)], 1)
    extra = np.zeros((16, 2 * LANES))
    extra[0, :LANES] = 1 - 2 * (np.arange(LANES) % 2)
    return two_parts(np.concatenate([table, extra], 0))


def y_inverse_table():
    part, row = row_order()
    column = np.arange(LANES)
    angle = 2 * np.pi / LANES * (row[:, None] * column[None, :] % LANES)
    cosine, sine = np.cos(angle), np.sin(angle)
    part, row = part[:, None], row[:, None]
    plain = np.concatenate([np.where(part == 0, cosine, -sine), np.where(part == 0, sine, cosine)], 1)
    sign = (1 - 2 * (column % 2))[None, :]
    first = np.where(part == 0, np.where(row == 0, 1.0, 2 * cosine), np.where(row == 0, sign, -2 * sine))
    return two_parts(np.concatenate([plain, first], 1) / (N * N))


def x_table(direction):
    line = np.arange(HALF)
    angle = 2 * np.pi / HALF * (line[:, None] * line[None, :] % HALF)
    both = np.eye(2)
    cosine, sine = np.kron(both, np.cos(angle)), direction * np.kron(both, np.sin(angle))
    return two_parts(np.block([[cosine, sine], [-sine, cosine]]))


def y_twist():
    angle = 2 * np.pi / N * (np.arange(16)[:, None] * np.arange(LANES)[None, :] % N)
    return np.stack([np.cos(angle), np.sin(angle)]).astype(np.float32)


def x_twist():
    half = np.arange(8)[None, :, None] // 4
    line = np.arange(16)[:, None, None]
    column = np.arange(LANES)[None, None, :] % HALF
    inner = 2 * np.pi / FFT * (half * line % FFT) * np.ones_like(column)
    outer = 2 * np.pi / N * ((2 * line + half) * column % N)
    return np.stack([np.cos(inner), np.sin(inner), np.cos(outer), np.sin(outer)]).astype(np.float32)


def x_choices():
    pick, spread = np.zeros((2, 5, FFT, LANES)), np.zeros((2, 5, 16, LANES))
    for sign in range(2):
        for p in range(FFT):
            for q in range(HALF):
                kx = p + FFT * q if sign == 0 else (N - p - FFT * q) % N
                case = 4 if sign == 1 and p == 0 and q % 4 == 0 else q % 4
                pick[sign, case, p % 2 * 16 + p // 2, kx % LANES] = 1
                spread[sign, case, kx // LANES, [q, HALF + q]] = 1
    return pick.reshape(2 * 5 * FFT, LANES).astype(ml_dtypes.bfloat16), spread.astype(ml_dtypes.bfloat16)


def split(values):
    high = values.astype(BF16)
    return high, (values - high.astype(F32)).astype(BF16)


def dot(left, right, dims):
    return lax.dot_general(left, right, (dims, ((), ())), preferred_element_type=F32)


def product(left, right, dims):
    (left_high, left_low), (right_high, right_low) = left, right
    return dot(left_high, right_high, dims) + (dot(left_low, right_high, dims) + dot(left_high, right_low, dims))


def turn(value, part, whole, direction):
    real, imag = value
    part = part % whole
    eighth = 8 * part
    if eighth % whole == 0:
        eighth = eighth // whole
        root = math.sqrt(0.5)
        if eighth == 0:
            return value
        if eighth == 4:
            return (-real, -imag)
        if eighth == 2 or eighth == 6:
            return (-imag, real) if (eighth == 2) == (direction > 0) else (imag, -real)
    cosine, sine = math.cos(2 * math.pi * part / whole), direction * math.sin(2 * math.pi * part / whole)
    return (real * cosine - imag * sine, real * sine + imag * cosine)


def plus(left, right):
    return (left[0] + right[0], left[1] + right[1])


def minus(left, right):
    return (left[0] - right[0], left[1] - right[1])


def small_dft(values, direction):
    size = len(values)
    if size == 1:
        return values
    even = small_dft(values[0::2], direction)
    odd = small_dft(values[1::2], direction)
    odd = [turn(odd[index], index, size, direction) for index in range(size // 2)]
    return [plus(even[index], odd[index]) for index in range(size // 2)] + [
        minus(even[index], odd[index]) for index in range(size // 2)
    ]


def dft16(real, imag, direction):
    shape = (4, 4) + real.shape[1:]
    real, imag = real.reshape(shape), imag.reshape(shape)
    first = small_dft([(real[u], imag[u]) for u in range(4)], direction)
    second = []
    for v in range(4):
        turned = [turn((first[w][0][v], first[w][1][v]), w * v, 16, direction) for w in range(4)]
        second.append((jnp.stack([value[0] for value in turned]), jnp.stack([value[1] for value in turned])))
    done = small_dft(second, direction)
    flat = (16,) + real.shape[2:]
    return (
        jnp.stack([value[0] for value in done]).reshape(flat),
        jnp.stack([value[1] for value in done]).reshape(flat),
    )


def real_dft(values):
    size = len(values)
    if size == 2:
        return [values[0] + values[1], values[0] - values[1]]
    even, odd = real_dft(values[0::2]), real_dft(values[1::2])
    half, quarter = size // 2, size // 4
    out = [None] * (half + 1)
    out[0], out[half] = even[0] + odd[0], even[0] - odd[0]
    out[quarter] = (even[quarter], -odd[quarter])
    for index in range(1, quarter):
        turned = turn(odd[index], index, size, -1)
        out[index] = plus(even[index], turned)
        back = minus(even[index], turned)
        out[half - index] = (back[0], -back[1])
    return out


def real_inverse(values):
    half = len(values) - 1
    size = 2 * half
    if size == 2:
        return [values[0] + values[1], values[0] - values[1]]
    quarter = size // 4
    even, odd = [None] * (quarter + 1), [None] * (quarter + 1)
    even[0], odd[0] = values[0] + values[half], values[0] - values[half]
    even[quarter], odd[quarter] = 2.0 * values[quarter][0], -2.0 * values[quarter][1]
    for index in range(1, quarter):
        mirror = (values[half - index][0], -values[half - index][1])
        even[index] = plus(values[index], mirror)
        odd[index] = turn(minus(values[index], mirror), index, size, 1)
    out = [None] * size
    out[0::2], out[1::2] = real_inverse(even), real_inverse(odd)
    return out


def y_operands(field, twist_cos, twist_sin):
    parts = real_dft([field[:, LANES * index : LANES * (index + 1)] for index in range(16)])
    sign = 1.0 - 2.0 * (lax.broadcasted_iota(jnp.int32, (OWN, LANES), 1) % 2).astype(F32)

    def twisted(index):
        cosine, sine = twist_cos[index][None, :], twist_sin[index][None, :]
        if index == 8:
            return jnp.concatenate([parts[8] * cosine, -parts[8] * sine], 1)
        real, imag = parts[index]
        return jnp.concatenate([real * cosine + imag * sine, imag * cosine - real * sine], 1)

    signs = jnp.concatenate([sign, sign], 1)
    out = [jnp.concatenate([jnp.concatenate([parts[0], jnp.zeros_like(parts[0])], 1), twisted(8)], 0)]
    for index in range(1, 8):
        value = twisted(index)
        out.append(jnp.concatenate([value, value * signs], 0))
    return out


def y_line(total, index, twist_cos, twist_sin):
    if index == 0:
        real, imag = total[OWN:, :LANES], total[OWN:, LANES : 2 * LANES]
        return total[:OWN, 2 * LANES :], 2.0 * (real * twist_cos[8][None, :] - imag * twist_sin[8][None, :])
    sign = 1.0 - 2.0 * (lax.broadcasted_iota(jnp.int32, (OWN, LANES), 1) % 2).astype(F32)
    real = total[:OWN, :LANES] + sign * total[OWN:, :LANES]
    imag = total[:OWN, LANES:] + sign * total[OWN:, LANES:]
    cosine, sine = twist_cos[index][None, :], twist_sin[index][None, :]
    return real * cosine - imag * sine, real * sine + imag * cosine


def y_result(lines):
    values = real_inverse([lines[0][0], *lines[1:], lines[0][1]])
    return [jnp.clip(value, -1.0, 1.0) for value in values]


def upper(shape):
    return lax.broadcasted_iota(jnp.int32, shape, 1) < 4


def x_forward(blocks, table, twist):
    total, rest = blocks[:16] + blocks[16:], blocks[:16] - blocks[16:]
    top = upper(total.shape)
    real = jnp.where(top, total, pltpu.roll(rest, 4, 1))
    imag = jnp.where(top, pltpu.roll(total, 4, 1), rest)
    real, imag = real * twist[0] + imag * twist[1], imag * twist[0] - real * twist[1]
    real, imag = dft16(real, imag, -1)
    both = jnp.concatenate([real * twist[2] + imag * twist[3], imag * twist[2] - real * twist[3]], 2)
    return product(split(both.reshape(LANES, 2 * LANES)), table, ((1,), (0,))).reshape(16, 8, 2 * LANES)


def x_inverse(values, table, twist):
    out = product(split(values.reshape(LANES, 2 * LANES)), table, ((1,), (0,))).reshape(16, 8, 2 * LANES)
    real, imag = out[:, :, :LANES], out[:, :, LANES:]
    real, imag = dft16(real * twist[2] - imag * twist[3], real * twist[3] + imag * twist[2], 1)
    real, imag = real * twist[0] - imag * twist[1], real * twist[1] + imag * twist[0]
    top = upper(real.shape)
    even = jnp.where(top, real, pltpu.roll(imag, 4, 1))
    odd = jnp.where(top, pltpu.roll(real, 4, 1), imag)
    return jnp.concatenate([even + odd, even - odd], 0)


def x_factors(shape, pick, spread):
    rest, parts = shape, []
    for _ in range(3):
        part = rest.astype(BF16)
        parts.append(part)
        rest = rest - part.astype(F32)
    chosen = [dot(pick, part, ((1,), (1,))).astype(BF16) for part in parts]
    out = []
    for sign in range(2):
        total = None
        for part in reversed(chosen):
            for case in range(4 + sign):
                start = FFT * (5 * sign + case)
                value = dot(part[start : start + FFT], spread[sign, case], ((1,), (0,)))
                total = value if total is None else total + value
        even, odd = total[:16, None, :], total[16:, None, :]
        out.append(jnp.where(upper((16, 8, LANES)), even, odd))
    return out


SEND, POWER, MEAN, BACK = range(4)


def far_first(step):
    return lax.rem(12 + (step + 1) // 2 * (1 - 2 * lax.rem(step, 2)), 8)


def kernel(
    field_hbm, yf_hbm, yi_hbm, xf_hbm, xi_hbm, yt_hbm, xt_hbm, pick_hbm, spread_hbm, xs_hbm, ys_hbm,
    out_hbm,
    field, yf, yi, xf, xi, yt, xt, pick, spread, xs, y_shape, out,
    sent, received, spec, power, powers, root, bound, back, returned, sym, lines,
    load_sem, send_sem, recv_sem,
):
    me = lax.axis_index("fft")
    plane = lax.axis_index("plane")
    other = plane + 1 - 2 * lax.rem(plane, 2)
    special = me == 0
    barrier = pltpu.get_barrier_semaphore()

    def fft_peer(step):
        return lax.rem(me // 4 + far_first(lax.rem(step, 8)), 8) * 4 + lax.rem(lax.rem(me, 4) + 1 + step // 8, 4)

    def plane_peer(step):
        return lax.rem(plane // 2 + far_first(step // 2), 8) * 2 + lax.rem(plane + 1 + step, 2)

    loads = []
    for index, (source, target) in enumerate(
        [
            (field_hbm, field), (yt_hbm, yt), (yf_hbm, yf), (ys_hbm, y_shape), (xs_hbm, xs), (pick_hbm, pick),
            (spread_hbm, spread), (xf_hbm, xf), (xt_hbm, xt), (xi_hbm, xi), (yi_hbm, yi),
        ]
    ):
        copy = pltpu.make_async_copy(source, target, load_sem.at[index])
        copy.start()
        loads.append(copy)

    @pl.loop(0, FFT)
    def _(step):
        pl.semaphore_signal(barrier, inc=1, device_id=(fft_peer(step), other), device_id_type=MESH)

    @pl.loop(0, PLANES - 1)
    def _(step):
        pl.semaphore_signal(barrier, inc=1, device_id=(me, plane_peer(step)), device_id_type=MESH)

    def all_to_all(source, target, chunk, kind):
        @pl.loop(0, FFT)
        def _(step):
            peer = fft_peer(step)
            pltpu.make_async_remote_copy(
                src_ref=source.at[chunk, peer],
                dst_ref=target.at[chunk, me],
                send_sem=send_sem.at[kind, chunk],
                recv_sem=recv_sem.at[kind, chunk],
                device_id=(peer, other),
                device_id_type=MESH,
            ).start()

    def to_planes(source, target, chunk, kind):
        @pl.loop(0, PLANES - 1)
        def _(step):
            peer = plane_peer(step)
            pltpu.make_async_remote_copy(
                src_ref=source(peer),
                dst_ref=target,
                send_sem=send_sem.at[kind, chunk],
                recv_sem=recv_sem.at[kind, chunk],
                device_id=(me, peer),
                device_id_type=MESH,
            ).start()

    def wait_for(ref, sem):
        pltpu.make_async_copy(ref, ref, sem).wait()

    for copy in loads[:3]:
        copy.wait()
    operands = y_operands(field[:, 0, :], yt[0], yt[1])
    for index, operand in enumerate(operands):
        operand = split(operand)
        done = product((yf[0, :128], yf[1, :128]), operand, ((1,), (1,)))
        if index == 0:
            extra = product((yf[0, 128:], yf[1, 128:]), operand, ((1,), (1,)))[0:1, :]
            row = lax.broadcasted_iota(jnp.int32, (128, LANES), 0)
            lane = lax.broadcasted_iota(jnp.int32, (128, LANES), 1)
            done = jnp.where((row == 4) & (lane < HALF), extra, done)
        first = 16 * (index % 2)
        sent[index // 2, first : first + 16] = done.reshape(16, 8, LANES)
        if index == 1:
            pl.semaphore_wait(barrier, FFT + PLANES - 1)
        if index % 2 == 1:
            all_to_all(sent, received, index // 2, SEND)

    for copy in loads[3:]:
        copy.wait()
    row = lax.broadcasted_iota(jnp.int32, (8, LANES), 0) % 4
    lane = lax.broadcasted_iota(jnp.int32, (8, LANES), 1)
    x_here, x_other = x_factors(xs[...], pick[...], spread[...])
    for chunk in range(CHUNKS):
        here, opposite = jnp.zeros((8, LANES), F32), jnp.zeros((8, LANES), F32)
        group = 2 * chunk + me // 16
        for half in range(2):
            for step in range(4):
                line = 4 * lax.rem(me, 16) + step
                ky = jnp.where(group == 0, 8 * half + 16 * line, group + 16 * (line + 64 * half))
                place = (row == step) & (lane // HALF == half)
                here = jnp.where(place, y_shape[ky], here)
                opposite = jnp.where(place, y_shape[lax.rem(N - ky, N)], opposite)
        bound[0, chunk] = here[None] * x_here
        bound[1, chunk] = opposite[None] * x_other

    @pl.when(special)
    def _():
        here = jnp.where(lane < HALF, y_shape[0], y_shape[N // 2])
        bound[0, SPECIAL] = here[None] * x_here
        bound[1, SPECIAL] = here[None] * x_other

    def along_x(blocks, chunk):
        done = x_forward(blocks, (xf[0], xf[1]), xt)
        spec[chunk] = done
        real, imag = done[:, :, :LANES], done[:, :, LANES:]
        power[chunk] = real * real + imag * imag
        powers[chunk, plane] = power[chunk, plane]
        to_planes(lambda peer: power.at[chunk, peer], powers.at[chunk, plane], chunk, POWER)

    def forward(chunk):
        wait_for(received.at[chunk], recv_sem.at[SEND, chunk])
        along_x(received[chunk], chunk)

    def average(chunk):
        wait_for(powers.at[chunk, pl.ds(0, PLANES - 1)], recv_sem.at[POWER, chunk])
        total = powers[chunk, 0]
        for index in range(1, PLANES):
            total = total + powers[chunk, index]
        root[chunk, plane] = jnp.sqrt(total * (1.0 / PLANES))
        to_planes(lambda peer: root.at[chunk, plane], root.at[chunk, plane], chunk, MEAN)

    def clipped(chunk):
        wait_for(root.at[chunk, pl.ds(0, PLANES - 1)], recv_sem.at[MEAN, chunk])
        here, opposite = bound[0, chunk] * root[chunk], bound[1, chunk] * root[chunk]
        real, imag = spec[chunk, :, :, :LANES], spec[chunk, :, :, LANES:]
        return [
            0.5 * (jnp.clip(value, -here, here) + jnp.clip(value, -opposite, opposite)) for value in (real, imag)
        ]

    def backward(chunk):
        real, imag = clipped(chunk)
        sym[:, :, :LANES] = real
        sym[:, :, LANES:] = imag
        if chunk == 0:

            @pl.when(special)
            def _():
                real, imag = clipped(SPECIAL)
                place = (row == 0)[None] & (lane < HALF)[None]
                sym[:, :, :LANES] = jnp.where(place, real - pltpu.roll(imag, HALF, 2), sym[:, :, :LANES])
                sym[:, :, LANES:] = jnp.where(place, imag + pltpu.roll(real, HALF, 2), sym[:, :, LANES:])

        back[chunk] = x_inverse(sym[...], (xi[0], xi[1]), xt)
        all_to_all(back, returned, chunk, BACK)

    def along_y(chunk):
        wait_for(returned.at[chunk], recv_sem.at[BACK, chunk])
        for index in (2 * chunk, 2 * chunk + 1):
            first = 16 * (index % 2)
            rows = returned[chunk, first : first + 16].reshape(LANES, LANES)
            width = 2 * LANES if index else 3 * LANES
            total = product(split(rows), (yi[0, :, :width], yi[1, :, :width]), ((0,), (0,)))
            lines[index, 0], lines[index, 1] = y_line(total, index, yt[0], yt[1])

    forward(0)

    @pl.when(special)
    def _():
        blocks = received[0]
        turned = pltpu.roll(pltpu.roll(blocks, HALF, 2), 4, 1)
        blocks = jnp.where((lane < HALF)[None], blocks, turned)
        along_x(jnp.where(upper(blocks.shape), blocks, 0.0), SPECIAL)

    forward(1)
    average(0)

    @pl.when(special)
    def _():
        average(SPECIAL)

    forward(2)
    average(1)
    backward(0)
    forward(3)
    average(2)
    backward(1)
    average(3)
    backward(2)
    backward(3)

    for chunk in range(CHUNKS):
        along_y(chunk)
    for index, value in enumerate(y_result([(lines[index, 0], lines[index, 1]) for index in range(8)])):
        out[:, 0, LANES * index : LANES * (index + 1)] = value
    store = pltpu.make_async_copy(out, out_hbm, load_sem.at[0])
    store.start()

    for chunk in range(CHUNKS):
        for kind in (SEND, BACK):
            wait_for(received.at[chunk], send_sem.at[kind, chunk])
        for kind in (POWER, MEAN):
            wait_for(powers.at[chunk, pl.ds(0, PLANES - 1)], send_sem.at[kind, chunk])

    @pl.when(special)
    def _():
        for kind in (POWER, MEAN):
            wait_for(powers.at[SPECIAL, pl.ds(0, PLANES - 1)], send_sem.at[kind, SPECIAL])

    store.wait()


def correct(error_field, x_shape, y_shape):
    shape = error_field.shape
    operands = [
        error_field, y_forward_table(), y_inverse_table(), x_table(-1), x_table(1), y_twist(), x_twist(), *x_choices(),
        x_shape.reshape(16, LANES), y_shape,
    ]
    operands = [jnp.asarray(operand) for operand in operands]
    inside = [pltpu.VMEM(operand.shape, operand.dtype) for operand in operands]
    inside[-1] = pltpu.SMEM(y_shape.shape, F32)
    outside = pl.BlockSpec(memory_space=pltpu.HBM)
    return pl.pallas_call(
        kernel,
        out_shape=jax.ShapeDtypeStruct(shape, F32),
        in_specs=[outside] * len(operands),
        out_specs=outside,
        scratch_shapes=inside
        + [
            pltpu.VMEM(shape, F32),
            pltpu.VMEM((CHUNKS, FFT, 8, LANES), F32),
            pltpu.VMEM((CHUNKS, FFT, 8, LANES), F32),
            pltpu.VMEM((CHUNKS + 1, 16, 8, 2 * LANES), F32),
            pltpu.VMEM((CHUNKS + 1, PLANES, 8, LANES), F32),
            pltpu.VMEM((CHUNKS + 1, PLANES, 8, LANES), F32),
            pltpu.VMEM((CHUNKS + 1, PLANES, 8, LANES), F32),
            pltpu.VMEM((2, CHUNKS + 1, 16, 8, LANES), F32),
            pltpu.VMEM((CHUNKS, FFT, 8, LANES), F32),
            pltpu.VMEM((CHUNKS, FFT, 8, LANES), F32),
            pltpu.VMEM((16, 8, 2 * LANES), F32),
            pltpu.VMEM((8, 2, OWN, LANES), F32),
            pltpu.SemaphoreType.DMA((len(operands),)),
            pltpu.SemaphoreType.DMA((4, CHUNKS + 1)),
            pltpu.SemaphoreType.DMA((4, CHUNKS + 1)),
        ],
        compiler_params=pltpu.CompilerParams(
            collective_id=0, has_side_effects=True, vmem_limit_bytes=63 * 1024 * 1024
        ),
    )(*operands)


def solution(mesh):
    placed = (P("fft", "plane", None), P(), P())
    return jax.shard_map(
        correct, mesh=mesh, in_specs=placed, out_specs=P("fft", "plane", None), check_vma=False
    )
```

```python
import math

import jax
import jax.numpy as jnp
import ml_dtypes
import numpy as np
from jax import lax
from jax.experimental import pallas as pl
from jax.experimental.pallas import tpu as pltpu
from jax.sharding import PartitionSpec as P

F32 = jnp.float32
BF16 = jnp.bfloat16
N = 2048
FFT = 32
PLANES = 16
OWN = N // FFT
HALF = 64
LANES = 128
CHUNKS = 4
SPECIAL = CHUNKS
MESH = pl.DeviceIdType.MESH


def two_parts(table):
    table = np.asarray(table, np.float64)
    high = table.astype(np.float32).astype(ml_dtypes.bfloat16)
    low = (table - high.astype(np.float64)).astype(np.float32).astype(ml_dtypes.bfloat16)
    return np.stack([high, low])


def row_order():
    block, part, step = np.meshgrid(np.arange(16), np.arange(2), np.arange(4), indexing="ij")
    return part.reshape(-1), (block * 4 + step).reshape(-1)


def y_forward_table():
    part, row = row_order()
    angle = 2 * np.pi / LANES * (row[:, None] * np.arange(LANES)[None, :] % LANES)
    cosine, sine = np.cos(angle), np.sin(angle)
    part = part[:, None]
    table = np.concatenate([np.where(part == 0, cosine, -sine), np.where(part == 0, sine, cosine)], 1)
    extra = np.zeros((16, 2 * LANES))
    extra[0, :LANES] = 1 - 2 * (np.arange(LANES) % 2)
    return two_parts(np.concatenate([table, extra], 0))


def y_inverse_table():
    part, row = row_order()
    column = np.arange(LANES)
    angle = 2 * np.pi / LANES * (row[:, None] * column[None, :] % LANES)
    cosine, sine = np.cos(angle), np.sin(angle)
    part, row = part[:, None], row[:, None]
    plain = np.concatenate([np.where(part == 0, cosine, -sine), np.where(part == 0, sine, cosine)], 1)
    sign = (1 - 2 * (column % 2))[None, :]
    first = np.where(part == 0, np.where(row == 0, 1.0, 2 * cosine), np.where(row == 0, sign, -2 * sine))
    return two_parts(np.concatenate([plain, first], 1) / (N * N))


def x_table(direction):
    line = np.arange(HALF)
    angle = 2 * np.pi / HALF * (line[:, None] * line[None, :] % HALF)
    both = np.eye(2)
    cosine, sine = np.kron(both, np.cos(angle)), direction * np.kron(both, np.sin(angle))
    return two_parts(np.block([[cosine, sine], [-sine, cosine]]))


def y_twist():
    angle = 2 * np.pi / N * (np.arange(16)[:, None] * np.arange(LANES)[None, :] % N)
    return np.stack([np.cos(angle), np.sin(angle)]).astype(np.float32)


def x_twist():
    half = np.arange(8)[None, :, None] // 4
    line = np.arange(16)[:, None, None]
    column = np.arange(LANES)[None, None, :] % HALF
    inner = 2 * np.pi / FFT * (half * line % FFT) * np.ones_like(column)
    outer = 2 * np.pi / N * ((2 * line + half) * column % N)
    return np.stack([np.cos(inner), np.sin(inner), np.cos(outer), np.sin(outer)]).astype(np.float32)


def x_choices():
    pick, spread = np.zeros((2, 5, FFT, LANES)), np.zeros((2, 5, 16, LANES))
    for sign in range(2):
        for p in range(FFT):
            for q in range(HALF):
                kx = p + FFT * q if sign == 0 else (N - p - FFT * q) % N
                case = 4 if sign == 1 and p == 0 and q % 4 == 0 else q % 4
                pick[sign, case, p % 2 * 16 + p // 2, kx % LANES] = 1
                spread[sign, case, kx // LANES, [q, HALF + q]] = 1
    return pick.reshape(2 * 5 * FFT, LANES).astype(ml_dtypes.bfloat16), spread.astype(ml_dtypes.bfloat16)


def split(values):
    high = values.astype(BF16)
    return high, (values - high.astype(F32)).astype(BF16)


def dot(left, right, dims):
    return lax.dot_general(left, right, (dims, ((), ())), preferred_element_type=F32)


def product(left, right, dims):
    (left_high, left_low), (right_high, right_low) = left, right
    return dot(left_high, right_high, dims) + (dot(left_low, right_high, dims) + dot(left_high, right_low, dims))


def turn(value, part, whole, direction):
    real, imag = value
    part = part % whole
    eighth = 8 * part
    if eighth % whole == 0:
        eighth = eighth // whole
        root = math.sqrt(0.5)
        if eighth == 0:
            return value
        if eighth == 4:
            return (-real, -imag)
        if eighth == 2 or eighth == 6:
            return (-imag, real) if (eighth == 2) == (direction > 0) else (imag, -real)
    cosine, sine = math.cos(2 * math.pi * part / whole), direction * math.sin(2 * math.pi * part / whole)
    return (real * cosine - imag * sine, real * sine + imag * cosine)


def plus(left, right):
    return (left[0] + right[0], left[1] + right[1])


def minus(left, right):
    return (left[0] - right[0], left[1] - right[1])


def small_dft(values, direction):
    size = len(values)
    if size == 1:
        return values
    even = small_dft(values[0::2], direction)
    odd = small_dft(values[1::2], direction)
    odd = [turn(odd[index], index, size, direction) for index in range(size // 2)]
    return [plus(even[index], odd[index]) for index in range(size // 2)] + [
        minus(even[index], odd[index]) for index in range(size // 2)
    ]


def dft16(real, imag, direction):
    shape = (4, 4) + real.shape[1:]
    real, imag = real.reshape(shape), imag.reshape(shape)
    first = small_dft([(real[u], imag[u]) for u in range(4)], direction)
    second = []
    for v in range(4):
        turned = [turn((first[w][0][v], first[w][1][v]), w * v, 16, direction) for w in range(4)]
        second.append((jnp.stack([value[0] for value in turned]), jnp.stack([value[1] for value in turned])))
    done = small_dft(second, direction)
    flat = (16,) + real.shape[2:]
    return (
        jnp.stack([value[0] for value in done]).reshape(flat),
        jnp.stack([value[1] for value in done]).reshape(flat),
    )


def real_dft(values):
    size = len(values)
    if size == 2:
        return [values[0] + values[1], values[0] - values[1]]
    even, odd = real_dft(values[0::2]), real_dft(values[1::2])
    half, quarter = size // 2, size // 4
    out = [None] * (half + 1)
    out[0], out[half] = even[0] + odd[0], even[0] - odd[0]
    out[quarter] = (even[quarter], -odd[quarter])
    for index in range(1, quarter):
        turned = turn(odd[index], index, size, -1)
        out[index] = plus(even[index], turned)
        back = minus(even[index], turned)
        out[half - index] = (back[0], -back[1])
    return out


def real_inverse(values):
    half = len(values) - 1
    size = 2 * half
    if size == 2:
        return [values[0] + values[1], values[0] - values[1]]
    quarter = size // 4
    even, odd = [None] * (quarter + 1), [None] * (quarter + 1)
    even[0], odd[0] = values[0] + values[half], values[0] - values[half]
    even[quarter], odd[quarter] = 2.0 * values[quarter][0], -2.0 * values[quarter][1]
    for index in range(1, quarter):
        mirror = (values[half - index][0], -values[half - index][1])
        even[index] = plus(values[index], mirror)
        odd[index] = turn(minus(values[index], mirror), index, size, 1)
    out = [None] * size
    out[0::2], out[1::2] = real_inverse(even), real_inverse(odd)
    return out


def y_operands(field, twist_cos, twist_sin):
    parts = real_dft(field)
    sign = 1.0 - 2.0 * (lax.broadcasted_iota(jnp.int32, (OWN, LANES), 1) % 2).astype(F32)

    def twisted(index):
        cosine, sine = twist_cos[index][None, :], twist_sin[index][None, :]
        if index == 8:
            return jnp.concatenate([parts[8] * cosine, -parts[8] * sine], 1)
        real, imag = parts[index]
        return jnp.concatenate([real * cosine + imag * sine, imag * cosine - real * sine], 1)

    signs = jnp.concatenate([sign, sign], 1)
    out = [jnp.concatenate([jnp.concatenate([parts[0], jnp.zeros_like(parts[0])], 1), twisted(8)], 0)]
    for index in range(1, 8):
        value = twisted(index)
        out.append(jnp.concatenate([value, value * signs], 0))
    return out


def y_line(total, index, twist_cos, twist_sin):
    if index == 0:
        real, imag = total[OWN:, :LANES], total[OWN:, LANES : 2 * LANES]
        return total[:OWN, 2 * LANES :], 2.0 * (real * twist_cos[8][None, :] - imag * twist_sin[8][None, :])
    sign = 1.0 - 2.0 * (lax.broadcasted_iota(jnp.int32, (OWN, LANES), 1) % 2).astype(F32)
    real = total[:OWN, :LANES] + sign * total[OWN:, :LANES]
    imag = total[:OWN, LANES:] + sign * total[OWN:, LANES:]
    cosine, sine = twist_cos[index][None, :], twist_sin[index][None, :]
    return real * cosine - imag * sine, real * sine + imag * cosine


def y_result(lines):
    values = real_inverse([lines[0][0], *lines[1:], lines[0][1]])
    return [jnp.clip(value, -1.0, 1.0) for value in values]


def upper(shape):
    return lax.broadcasted_iota(jnp.int32, shape, 1) < 4


def x_forward(blocks, table, twist):
    total, rest = blocks[:16] + blocks[16:], blocks[:16] - blocks[16:]
    top = upper(total.shape)
    real = jnp.where(top, total, pltpu.roll(rest, 4, 1))
    imag = jnp.where(top, pltpu.roll(total, 4, 1), rest)
    real, imag = real * twist[0] + imag * twist[1], imag * twist[0] - real * twist[1]
    real, imag = dft16(real, imag, -1)
    both = jnp.concatenate([real * twist[2] + imag * twist[3], imag * twist[2] - real * twist[3]], 2)
    return product(split(both.reshape(LANES, 2 * LANES)), table, ((1,), (0,))).reshape(16, 8, 2 * LANES)


def x_inverse(values, table, twist):
    out = product(split(values.reshape(LANES, 2 * LANES)), table, ((1,), (0,))).reshape(16, 8, 2 * LANES)
    real, imag = out[:, :, :LANES], out[:, :, LANES:]
    real, imag = dft16(real * twist[2] - imag * twist[3], real * twist[3] + imag * twist[2], 1)
    real, imag = real * twist[0] - imag * twist[1], real * twist[1] + imag * twist[0]
    top = upper(real.shape)
    even = jnp.where(top, real, pltpu.roll(imag, 4, 1))
    odd = jnp.where(top, pltpu.roll(real, 4, 1), imag)
    return jnp.concatenate([even + odd, even - odd], 0)


def x_factors(shape, pick, spread):
    rest, parts = shape, []
    for _ in range(3):
        part = rest.astype(BF16)
        parts.append(part)
        rest = rest - part.astype(F32)
    chosen = [dot(pick, part, ((1,), (1,))).astype(BF16) for part in parts]
    out = []
    for sign in range(2):
        total = None
        for part in reversed(chosen):
            for case in range(4 + sign):
                start = FFT * (5 * sign + case)
                value = dot(part[start : start + FFT], spread[sign, case], ((1,), (0,)))
                total = value if total is None else total + value
        even, odd = total[:16, None, :], total[16:, None, :]
        out.append(jnp.where(upper((16, 8, LANES)), even, odd))
    return out


SEND, POWER, MEAN, BACK = range(4)


def far_first(step):
    return lax.rem(12 + (step + 1) // 2 * (1 - 2 * lax.rem(step, 2)), 8)


def kernel(
    field_hbm, yf_hbm, yi_hbm, xf_hbm, xi_hbm, yt_hbm, xt_hbm, pick_hbm, spread_hbm, xs_hbm, ys_hbm,
    out,
    field, yf, yi, xf, xi, yt, xt, pick, spread, xs, y_shape,
    sent, received, spec, power, powers, root, bound, back, returned, sym, lines,
    load_sem, send_sem, recv_sem,
):
    me = lax.axis_index("fft")
    plane = lax.axis_index("plane")
    other = plane + 1 - 2 * lax.rem(plane, 2)
    special = me == 0
    barrier = pltpu.get_barrier_semaphore()

    def fft_peer(step):
        return lax.rem(me // 4 + far_first(lax.rem(step, 8)), 8) * 4 + lax.rem(lax.rem(me, 4) + 1 + step // 8, 4)

    def plane_peer(step):
        return lax.rem(plane // 2 + far_first(step // 2), 8) * 2 + lax.rem(plane + 1 + step, 2)

    loads = []
    for index, (source, target) in enumerate(
        [
            (field_hbm, field), (yt_hbm, yt), (yf_hbm, yf), (ys_hbm, y_shape), (xs_hbm, xs), (pick_hbm, pick),
            (spread_hbm, spread), (xf_hbm, xf), (xt_hbm, xt), (xi_hbm, xi), (yi_hbm, yi),
        ]
    ):
        copy = pltpu.make_async_copy(source, target, load_sem.at[index])
        copy.start()
        loads.append(copy)

    @pl.loop(0, FFT)
    def _(step):
        pl.semaphore_signal(barrier, inc=1, device_id=(fft_peer(step), other), device_id_type=MESH)

    @pl.loop(0, PLANES - 1)
    def _(step):
        pl.semaphore_signal(barrier, inc=1, device_id=(me, plane_peer(step)), device_id_type=MESH)

    def all_to_all(source, target, chunk, kind):
        @pl.loop(0, FFT)
        def _(step):
            peer = fft_peer(step)
            pltpu.make_async_remote_copy(
                src_ref=source.at[chunk, peer],
                dst_ref=target.at[chunk, me],
                send_sem=send_sem.at[kind, chunk],
                recv_sem=recv_sem.at[kind, chunk],
                device_id=(peer, other),
                device_id_type=MESH,
            ).start()

    def to_planes(source, target, chunk, kind):
        @pl.loop(0, PLANES - 1)
        def _(step):
            peer = plane_peer(step)
            pltpu.make_async_remote_copy(
                src_ref=source(peer),
                dst_ref=target,
                send_sem=send_sem.at[kind, chunk],
                recv_sem=recv_sem.at[kind, chunk],
                device_id=(me, peer),
                device_id_type=MESH,
            ).start()

    def wait_for(ref, sem):
        pltpu.make_async_copy(ref, ref, sem).wait()

    for copy in loads[:3]:
        copy.wait()
    operands = y_operands([field[:, index, :] for index in range(16)], yt[0], yt[1])
    for index, operand in enumerate(operands):
        operand = split(operand)
        done = product((yf[0, :128], yf[1, :128]), operand, ((1,), (1,)))
        if index == 0:
            extra = product((yf[0, 128:], yf[1, 128:]), operand, ((1,), (1,)))[0:1, :]
            row = lax.broadcasted_iota(jnp.int32, (128, LANES), 0)
            lane = lax.broadcasted_iota(jnp.int32, (128, LANES), 1)
            done = jnp.where((row == 4) & (lane < HALF), extra, done)
        first = 16 * (index % 2)
        sent[index // 2, first : first + 16] = done.reshape(16, 8, LANES)
        if index == 1:
            pl.semaphore_wait(barrier, FFT + PLANES - 1)
        if index % 2 == 1:
            all_to_all(sent, received, index // 2, SEND)

    for copy in loads[3:]:
        copy.wait()
    row = lax.broadcasted_iota(jnp.int32, (8, LANES), 0) % 4
    lane = lax.broadcasted_iota(jnp.int32, (8, LANES), 1)
    x_here, x_other = x_factors(xs[...], pick[...], spread[...])
    for chunk in range(CHUNKS):
        here, opposite = jnp.zeros((8, LANES), F32), jnp.zeros((8, LANES), F32)
        group = 2 * chunk + me // 16
        for half in range(2):
            for step in range(4):
                line = 4 * lax.rem(me, 16) + step
                ky = jnp.where(group == 0, 8 * half + 16 * line, group + 16 * (line + 64 * half))
                place = (row == step) & (lane // HALF == half)
                here = jnp.where(place, y_shape[ky], here)
                opposite = jnp.where(place, y_shape[lax.rem(N - ky, N)], opposite)
        bound[0, chunk] = here[None] * x_here
        bound[1, chunk] = opposite[None] * x_other

    @pl.when(special)
    def _():
        here = jnp.where(lane < HALF, y_shape[0], y_shape[N // 2])
        bound[0, SPECIAL] = here[None] * x_here
        bound[1, SPECIAL] = here[None] * x_other

    def along_x(blocks, chunk):
        done = x_forward(blocks, (xf[0], xf[1]), xt)
        spec[chunk] = done
        real, imag = done[:, :, :LANES], done[:, :, LANES:]
        power[chunk] = real * real + imag * imag
        powers[chunk, plane] = power[chunk, plane]
        to_planes(lambda peer: power.at[chunk, peer], powers.at[chunk, plane], chunk, POWER)

    def forward(chunk):
        wait_for(received.at[chunk], recv_sem.at[SEND, chunk])
        along_x(received[chunk], chunk)

    def average(chunk):
        wait_for(powers.at[chunk, pl.ds(0, PLANES - 1)], recv_sem.at[POWER, chunk])
        total = powers[chunk, 0]
        for index in range(1, PLANES):
            total = total + powers[chunk, index]
        root[chunk, plane] = jnp.sqrt(total * (1.0 / PLANES))
        to_planes(lambda peer: root.at[chunk, plane], root.at[chunk, plane], chunk, MEAN)

    def clipped(chunk):
        wait_for(root.at[chunk, pl.ds(0, PLANES - 1)], recv_sem.at[MEAN, chunk])
        here, opposite = bound[0, chunk] * root[chunk], bound[1, chunk] * root[chunk]
        real, imag = spec[chunk, :, :, :LANES], spec[chunk, :, :, LANES:]
        return [
            0.5 * (jnp.clip(value, -here, here) + jnp.clip(value, -opposite, opposite)) for value in (real, imag)
        ]

    def backward(chunk):
        real, imag = clipped(chunk)
        sym[:, :, :LANES] = real
        sym[:, :, LANES:] = imag
        if chunk == 0:

            @pl.when(special)
            def _():
                real, imag = clipped(SPECIAL)
                place = (row == 0)[None] & (lane < HALF)[None]
                sym[:, :, :LANES] = jnp.where(place, real - pltpu.roll(imag, HALF, 2), sym[:, :, :LANES])
                sym[:, :, LANES:] = jnp.where(place, imag + pltpu.roll(real, HALF, 2), sym[:, :, LANES:])

        back[chunk] = x_inverse(sym[...], (xi[0], xi[1]), xt)
        all_to_all(back, returned, chunk, BACK)

    def along_y(chunk):
        wait_for(returned.at[chunk], recv_sem.at[BACK, chunk])
        for index in (2 * chunk, 2 * chunk + 1):
            first = 16 * (index % 2)
            rows = returned[chunk, first : first + 16].reshape(LANES, LANES)
            width = 2 * LANES if index else 3 * LANES
            total = product(split(rows), (yi[0, :, :width], yi[1, :, :width]), ((0,), (0,)))
            lines[index, 0], lines[index, 1] = y_line(total, index, yt[0], yt[1])

    forward(0)

    @pl.when(special)
    def _():
        blocks = received[0]
        turned = pltpu.roll(pltpu.roll(blocks, HALF, 2), 4, 1)
        blocks = jnp.where((lane < HALF)[None], blocks, turned)
        along_x(jnp.where(upper(blocks.shape), blocks, 0.0), SPECIAL)

    forward(1)
    average(0)

    @pl.when(special)
    def _():
        average(SPECIAL)

    forward(2)
    average(1)
    forward(3)
    backward(0)
    average(2)
    backward(1)
    average(3)
    backward(2)
    backward(3)

    for chunk in range(CHUNKS):
        along_y(chunk)
    for index, value in enumerate(y_result([(lines[index, 0], lines[index, 1]) for index in range(8)])):
        out[:, index, :] = value

    for chunk in range(CHUNKS):
        for kind in (SEND, BACK):
            wait_for(received.at[chunk], send_sem.at[kind, chunk])
        for kind in (POWER, MEAN):
            wait_for(powers.at[chunk, pl.ds(0, PLANES - 1)], send_sem.at[kind, chunk])

    @pl.when(special)
    def _():
        for kind in (POWER, MEAN):
            wait_for(powers.at[SPECIAL, pl.ds(0, PLANES - 1)], send_sem.at[kind, SPECIAL])


def correct(error_field, x_shape, y_shape):
    shape = (OWN, 16, LANES)
    operands = [
        error_field.reshape(shape), y_forward_table(), y_inverse_table(), x_table(-1), x_table(1), y_twist(), x_twist(), *x_choices(),
        x_shape.reshape(16, LANES), y_shape,
    ]
    operands = [jnp.asarray(operand) for operand in operands]
    inside = [pltpu.VMEM(operand.shape, operand.dtype) for operand in operands]
    inside[-1] = pltpu.SMEM(y_shape.shape, F32)
    outside = pl.BlockSpec(memory_space=pltpu.HBM)
    done = pl.pallas_call(
        kernel,
        out_shape=pltpu.VMEM(shape, F32),
        in_specs=[outside] * len(operands),
        out_specs=pl.BlockSpec(memory_space=pltpu.VMEM),
        scratch_shapes=inside
        + [
            pltpu.VMEM((CHUNKS, FFT, 8, LANES), F32),
            pltpu.VMEM((CHUNKS, FFT, 8, LANES), F32),
            pltpu.VMEM((CHUNKS + 1, 16, 8, 2 * LANES), F32),
            pltpu.VMEM((CHUNKS + 1, PLANES, 8, LANES), F32),
            pltpu.VMEM((CHUNKS + 1, PLANES, 8, LANES), F32),
            pltpu.VMEM((CHUNKS + 1, PLANES, 8, LANES), F32),
            pltpu.VMEM((2, CHUNKS + 1, 16, 8, LANES), F32),
            pltpu.VMEM((CHUNKS, FFT, 8, LANES), F32),
            pltpu.VMEM((CHUNKS, FFT, 8, LANES), F32),
            pltpu.VMEM((16, 8, 2 * LANES), F32),
            pltpu.VMEM((8, 2, OWN, LANES), F32),
            pltpu.SemaphoreType.DMA((len(operands),)),
            pltpu.SemaphoreType.DMA((4, CHUNKS + 1)),
            pltpu.SemaphoreType.DMA((4, CHUNKS + 1)),
        ],
        compiler_params=pltpu.CompilerParams(
            collective_id=0, has_side_effects=True, vmem_limit_bytes=60 * 1024 * 1024
        ),
    )(*operands)
    return done.reshape(error_field.shape)


def solution(mesh):
    placed = (P("fft", "plane", None), P(), P())
    return jax.shard_map(
        correct, mesh=mesh, in_specs=placed, out_specs=P("fft", "plane", None), check_vma=False
    )
```

```python
import math

import jax
import jax.numpy as jnp
import ml_dtypes
import numpy as np
from jax import lax
from jax.experimental import pallas as pl
from jax.experimental.pallas import tpu as pltpu
from jax.sharding import PartitionSpec as P

F32 = jnp.float32
BF16 = jnp.bfloat16
N = 2048
FFT = 32
PLANES = 16
OWN = N // FFT
HALF = 64
LANES = 128
CHUNKS = 4
SPECIAL = CHUNKS
MESH = pl.DeviceIdType.MESH


def two_parts(table):
    table = np.asarray(table, np.float64)
    high = table.astype(np.float32).astype(ml_dtypes.bfloat16)
    low = (table - high.astype(np.float64)).astype(np.float32).astype(ml_dtypes.bfloat16)
    return np.stack([high, low])


def row_order():
    block, part, step = np.meshgrid(np.arange(16), np.arange(2), np.arange(4), indexing="ij")
    return part.reshape(-1), (block * 4 + step).reshape(-1)


def y_forward_table():
    part, row = row_order()
    angle = 2 * np.pi / LANES * (row[:, None] * np.arange(LANES)[None, :] % LANES)
    cosine, sine = np.cos(angle), np.sin(angle)
    part = part[:, None]
    table = np.concatenate([np.where(part == 0, cosine, -sine), np.where(part == 0, sine, cosine)], 1)
    extra = np.zeros((16, 2 * LANES))
    extra[0, :LANES] = 1 - 2 * (np.arange(LANES) % 2)
    return two_parts(np.concatenate([table, extra], 0))


def y_inverse_table():
    part, row = row_order()
    column = np.arange(LANES)
    angle = 2 * np.pi / LANES * (row[:, None] * column[None, :] % LANES)
    cosine, sine = np.cos(angle), np.sin(angle)
    part, row = part[:, None], row[:, None]
    plain = np.concatenate([np.where(part == 0, cosine, -sine), np.where(part == 0, sine, cosine)], 1)
    sign = (1 - 2 * (column % 2))[None, :]
    first = np.where(part == 0, np.where(row == 0, 1.0, 2 * cosine), np.where(row == 0, sign, -2 * sine))
    return two_parts(np.concatenate([plain, first], 1) / (N * N))


def x_table(direction):
    line = np.arange(HALF)
    angle = 2 * np.pi / HALF * (line[:, None] * line[None, :] % HALF)
    both = np.eye(2)
    cosine, sine = np.kron(both, np.cos(angle)), direction * np.kron(both, np.sin(angle))
    return two_parts(np.block([[cosine, sine], [-sine, cosine]]))


def y_twist():
    angle = 2 * np.pi / N * (np.arange(16)[:, None] * np.arange(LANES)[None, :] % N)
    return np.stack([np.cos(angle), np.sin(angle)]).astype(np.float32)


def x_twist():
    half = np.arange(8)[None, :, None] // 4
    line = np.arange(16)[:, None, None]
    column = np.arange(LANES)[None, None, :] % HALF
    inner = 2 * np.pi / FFT * (half * line % FFT) * np.ones_like(column)
    outer = 2 * np.pi / N * ((2 * line + half) * column % N)
    return np.stack([np.cos(inner), np.sin(inner), np.cos(outer), np.sin(outer)]).astype(np.float32)


def x_choices():
    pick, spread = np.zeros((2, 5, FFT, LANES)), np.zeros((2, 5, 16, LANES))
    for sign in range(2):
        for p in range(FFT):
            for q in range(HALF):
                kx = p + FFT * q if sign == 0 else (N - p - FFT * q) % N
                case = 4 if sign == 1 and p == 0 and q % 4 == 0 else q % 4
                pick[sign, case, p % 2 * 16 + p // 2, kx % LANES] = 1
                spread[sign, case, kx // LANES, [q, HALF + q]] = 1
    return pick.reshape(2 * 5 * FFT, LANES).astype(ml_dtypes.bfloat16), spread.astype(ml_dtypes.bfloat16)


def split(values):
    high = values.astype(BF16)
    return high, (values - high.astype(F32)).astype(BF16)


def dot(left, right, dims):
    return lax.dot_general(left, right, (dims, ((), ())), preferred_element_type=F32)


def product(left, right, dims):
    (left_high, left_low), (right_high, right_low) = left, right
    return dot(left_high, right_high, dims) + (dot(left_low, right_high, dims) + dot(left_high, right_low, dims))


def turn(value, part, whole, direction):
    real, imag = value
    part = part % whole
    eighth = 8 * part
    if eighth % whole == 0:
        eighth = eighth // whole
        root = math.sqrt(0.5)
        if eighth == 0:
            return value
        if eighth == 4:
            return (-real, -imag)
        if eighth == 2 or eighth == 6:
            return (-imag, real) if (eighth == 2) == (direction > 0) else (imag, -real)
    cosine, sine = math.cos(2 * math.pi * part / whole), direction * math.sin(2 * math.pi * part / whole)
    return (real * cosine - imag * sine, real * sine + imag * cosine)


def plus(left, right):
    return (left[0] + right[0], left[1] + right[1])


def minus(left, right):
    return (left[0] - right[0], left[1] - right[1])


def small_dft(values, direction):
    size = len(values)
    if size == 1:
        return values
    even = small_dft(values[0::2], direction)
    odd = small_dft(values[1::2], direction)
    odd = [turn(odd[index], index, size, direction) for index in range(size // 2)]
    return [plus(even[index], odd[index]) for index in range(size // 2)] + [
        minus(even[index], odd[index]) for index in range(size // 2)
    ]


def dft16(real, imag, direction):
    shape = (4, 4) + real.shape[1:]
    real, imag = real.reshape(shape), imag.reshape(shape)
    first = small_dft([(real[u], imag[u]) for u in range(4)], direction)
    second = []
    for v in range(4):
        turned = [turn((first[w][0][v], first[w][1][v]), w * v, 16, direction) for w in range(4)]
        second.append((jnp.stack([value[0] for value in turned]), jnp.stack([value[1] for value in turned])))
    done = small_dft(second, direction)
    flat = (16,) + real.shape[2:]
    return (
        jnp.stack([value[0] for value in done]).reshape(flat),
        jnp.stack([value[1] for value in done]).reshape(flat),
    )


def real_dft(values):
    size = len(values)
    if size == 2:
        return [values[0] + values[1], values[0] - values[1]]
    even, odd = real_dft(values[0::2]), real_dft(values[1::2])
    half, quarter = size // 2, size // 4
    out = [None] * (half + 1)
    out[0], out[half] = even[0] + odd[0], even[0] - odd[0]
    out[quarter] = (even[quarter], -odd[quarter])
    for index in range(1, quarter):
        turned = turn(odd[index], index, size, -1)
        out[index] = plus(even[index], turned)
        back = minus(even[index], turned)
        out[half - index] = (back[0], -back[1])
    return out


def real_inverse(values):
    half = len(values) - 1
    size = 2 * half
    if size == 2:
        return [values[0] + values[1], values[0] - values[1]]
    quarter = size // 4
    even, odd = [None] * (quarter + 1), [None] * (quarter + 1)
    even[0], odd[0] = values[0] + values[half], values[0] - values[half]
    even[quarter], odd[quarter] = 2.0 * values[quarter][0], -2.0 * values[quarter][1]
    for index in range(1, quarter):
        mirror = (values[half - index][0], -values[half - index][1])
        even[index] = plus(values[index], mirror)
        odd[index] = turn(minus(values[index], mirror), index, size, 1)
    out = [None] * size
    out[0::2], out[1::2] = real_inverse(even), real_inverse(odd)
    return out


def y_operands(field, twist_cos, twist_sin):
    parts = real_dft(field)
    sign = 1.0 - 2.0 * (lax.broadcasted_iota(jnp.int32, (OWN, LANES), 1) % 2).astype(F32)

    def twisted(index):
        cosine, sine = twist_cos[index][None, :], twist_sin[index][None, :]
        if index == 8:
            return jnp.concatenate([parts[8] * cosine, -parts[8] * sine], 1)
        real, imag = parts[index]
        return jnp.concatenate([real * cosine + imag * sine, imag * cosine - real * sine], 1)

    signs = jnp.concatenate([sign, sign], 1)
    out = [jnp.concatenate([jnp.concatenate([parts[0], jnp.zeros_like(parts[0])], 1), twisted(8)], 0)]
    for index in range(1, 8):
        value = twisted(index)
        out.append(jnp.concatenate([value, value * signs], 0))
    return out


def y_line(total, index, twist_cos, twist_sin):
    if index == 0:
        real, imag = total[OWN:, :LANES], total[OWN:, LANES : 2 * LANES]
        return total[:OWN, 2 * LANES :], 2.0 * (real * twist_cos[8][None, :] - imag * twist_sin[8][None, :])
    sign = 1.0 - 2.0 * (lax.broadcasted_iota(jnp.int32, (OWN, LANES), 1) % 2).astype(F32)
    real = total[:OWN, :LANES] + sign * total[OWN:, :LANES]
    imag = total[:OWN, LANES:] + sign * total[OWN:, LANES:]
    cosine, sine = twist_cos[index][None, :], twist_sin[index][None, :]
    return real * cosine - imag * sine, real * sine + imag * cosine


def y_result(lines):
    values = real_inverse([lines[0][0], *lines[1:], lines[0][1]])
    return [jnp.clip(value, -1.0, 1.0) for value in values]


def upper(shape):
    return lax.broadcasted_iota(jnp.int32, shape, 1) < 4


def x_forward(blocks, table, twist):
    total, rest = blocks[:16] + blocks[16:], blocks[:16] - blocks[16:]
    top = upper(total.shape)
    real = jnp.where(top, total, pltpu.roll(rest, 4, 1))
    imag = jnp.where(top, pltpu.roll(total, 4, 1), rest)
    real, imag = real * twist[0] + imag * twist[1], imag * twist[0] - real * twist[1]
    real, imag = dft16(real, imag, -1)
    both = jnp.concatenate([real * twist[2] + imag * twist[3], imag * twist[2] - real * twist[3]], 2)
    return product(split(both.reshape(LANES, 2 * LANES)), table, ((1,), (0,))).reshape(16, 8, 2 * LANES)


def x_inverse(values, table, twist):
    out = product(split(values.reshape(LANES, 2 * LANES)), table, ((1,), (0,))).reshape(16, 8, 2 * LANES)
    real, imag = out[:, :, :LANES], out[:, :, LANES:]
    real, imag = dft16(real * twist[2] - imag * twist[3], real * twist[3] + imag * twist[2], 1)
    real, imag = real * twist[0] - imag * twist[1], real * twist[1] + imag * twist[0]
    top = upper(real.shape)
    even = jnp.where(top, real, pltpu.roll(imag, 4, 1))
    odd = jnp.where(top, pltpu.roll(real, 4, 1), imag)
    return jnp.concatenate([even + odd, even - odd], 0)


def x_factors(shape, pick, spread):
    rest, parts = shape, []
    for _ in range(3):
        part = rest.astype(BF16)
        parts.append(part)
        rest = rest - part.astype(F32)
    chosen = [dot(pick, part, ((1,), (1,))).astype(BF16) for part in parts]
    out = []
    for sign in range(2):
        total = None
        for part in reversed(chosen):
            for case in range(4 + sign):
                start = FFT * (5 * sign + case)
                value = dot(part[start : start + FFT], spread[sign, case], ((1,), (0,)))
                total = value if total is None else total + value
        even, odd = total[:16, None, :], total[16:, None, :]
        out.append(jnp.where(upper((16, 8, LANES)), even, odd))
    return out


SEND, POWER, MEAN, BACK = range(4)


def far_first(step):
    return lax.rem(12 + (step + 1) // 2 * (1 - 2 * lax.rem(step, 2)), 8)


def kernel(
    field_hbm, yf_hbm, yi_hbm, xf_hbm, xi_hbm, yt_hbm, xt_hbm, pick_hbm, spread_hbm, xs_hbm, ys_hbm,
    out,
    field, yf, yi, xf, xi, yt, xt, pick, spread, xs, y_shape,
    sent, received, spec, power, powers, root, bound, back, returned, sym, lines,
    load_sem, send_sem, recv_sem,
):
    me = lax.axis_index("fft")
    plane = lax.axis_index("plane")
    other = plane + 1 - 2 * lax.rem(plane, 2)
    special = me == 0
    barrier = pltpu.get_barrier_semaphore()

    def fft_peer(step):
        part = step // 8
        place = 2 * lax.rem(lax.rem(me, 4) // 2 + 1 + part, 2) + part // 2
        return lax.rem(me // 4 + far_first(lax.rem(step, 8)), 8) * 4 + place

    def plane_peer(step):
        return lax.rem(plane // 2 + far_first(step // 2), 8) * 2 + lax.rem(plane + 1 + step, 2)

    loads = []
    for index, (source, target) in enumerate(
        [
            (field_hbm, field), (yt_hbm, yt), (yf_hbm, yf), (ys_hbm, y_shape), (xs_hbm, xs), (pick_hbm, pick),
            (spread_hbm, spread), (xf_hbm, xf), (xt_hbm, xt), (xi_hbm, xi), (yi_hbm, yi),
        ]
    ):
        loads.append(pltpu.make_async_copy(source, target, load_sem.at[index]))
    for copy in loads[:3]:
        copy.start()

    @pl.loop(0, FFT)
    def _(step):
        pl.semaphore_signal(barrier, inc=1, device_id=(fft_peer(step), other), device_id_type=MESH)

    @pl.loop(0, PLANES - 1)
    def _(step):
        pl.semaphore_signal(barrier, inc=1, device_id=(me, plane_peer(step)), device_id_type=MESH)

    for copy in loads[3:]:
        copy.start()

    def all_to_all(source, target, chunk, kind):
        @pl.loop(0, FFT)
        def _(step):
            peer = fft_peer(step)
            pltpu.make_async_remote_copy(
                src_ref=source.at[chunk, peer],
                dst_ref=target.at[chunk, me],
                send_sem=send_sem.at[kind, chunk],
                recv_sem=recv_sem.at[kind, chunk],
                device_id=(peer, other),
                device_id_type=MESH,
            ).start()

    def to_planes(source, target, chunk, kind):
        @pl.loop(0, PLANES - 1)
        def _(step):
            peer = plane_peer(step)
            pltpu.make_async_remote_copy(
                src_ref=source(peer),
                dst_ref=target,
                send_sem=send_sem.at[kind, chunk],
                recv_sem=recv_sem.at[kind, chunk],
                device_id=(me, peer),
                device_id_type=MESH,
            ).start()

    def wait_for(ref, sem):
        pltpu.make_async_copy(ref, ref, sem).wait()

    for copy in loads[:3]:
        copy.wait()
    operands = y_operands([field[:, index, :] for index in range(16)], yt[0], yt[1])
    for index, operand in enumerate(operands):
        operand = split(operand)
        done = product((yf[0, :128], yf[1, :128]), operand, ((1,), (1,)))
        if index == 0:
            extra = product((yf[0, 128:], yf[1, 128:]), operand, ((1,), (1,)))[0:1, :]
            row = lax.broadcasted_iota(jnp.int32, (128, LANES), 0)
            lane = lax.broadcasted_iota(jnp.int32, (128, LANES), 1)
            done = jnp.where((row == 4) & (lane < HALF), extra, done)
        first = 16 * (index % 2)
        sent[index // 2, first : first + 16] = done.reshape(16, 8, LANES)
        if index == 1:
            pl.semaphore_wait(barrier, FFT + PLANES - 1)
        if index % 2 == 1:
            all_to_all(sent, received, index // 2, SEND)

    for copy in loads[3:]:
        copy.wait()
    row = lax.broadcasted_iota(jnp.int32, (8, LANES), 0) % 4
    lane = lax.broadcasted_iota(jnp.int32, (8, LANES), 1)
    x_here, x_other = x_factors(xs[...], pick[...], spread[...])
    for chunk in range(CHUNKS):
        here, opposite = jnp.zeros((8, LANES), F32), jnp.zeros((8, LANES), F32)
        group = 2 * chunk + me // 16
        for half in range(2):
            for step in range(4):
                line = 4 * lax.rem(me, 16) + step
                ky = jnp.where(group == 0, 8 * half + 16 * line, group + 16 * (line + 64 * half))
                place = (row == step) & (lane // HALF == half)
                here = jnp.where(place, y_shape[ky], here)
                opposite = jnp.where(place, y_shape[lax.rem(N - ky, N)], opposite)
        bound[0, chunk] = here[None] * x_here
        bound[1, chunk] = opposite[None] * x_other

    @pl.when(special)
    def _():
        here = jnp.where(lane < HALF, y_shape[0], y_shape[N // 2])
        bound[0, SPECIAL] = here[None] * x_here
        bound[1, SPECIAL] = here[None] * x_other

    def along_x(blocks, chunk):
        done = x_forward(blocks, (xf[0], xf[1]), xt)
        spec[chunk] = done
        real, imag = done[:, :, :LANES], done[:, :, LANES:]
        power[chunk] = real * real + imag * imag
        powers[chunk, plane] = power[chunk, plane]
        to_planes(lambda peer: power.at[chunk, peer], powers.at[chunk, plane], chunk, POWER)

    def forward(chunk):
        wait_for(received.at[chunk], recv_sem.at[SEND, chunk])
        along_x(received[chunk], chunk)

    def average(chunk):
        wait_for(powers.at[chunk, pl.ds(0, PLANES - 1)], recv_sem.at[POWER, chunk])
        total = powers[chunk, 0]
        for index in range(1, PLANES):
            total = total + powers[chunk, index]
        root[chunk, plane] = jnp.sqrt(total * (1.0 / PLANES))
        to_planes(lambda peer: root.at[chunk, plane], root.at[chunk, plane], chunk, MEAN)

    def clipped(chunk):
        wait_for(root.at[chunk, pl.ds(0, PLANES - 1)], recv_sem.at[MEAN, chunk])
        here, opposite = bound[0, chunk] * root[chunk], bound[1, chunk] * root[chunk]
        real, imag = spec[chunk, :, :, :LANES], spec[chunk, :, :, LANES:]
        return [
            0.5 * (jnp.clip(value, -here, here) + jnp.clip(value, -opposite, opposite)) for value in (real, imag)
        ]

    def backward(chunk):
        real, imag = clipped(chunk)
        sym[:, :, :LANES] = real
        sym[:, :, LANES:] = imag
        if chunk == 0:

            @pl.when(special)
            def _():
                real, imag = clipped(SPECIAL)
                place = (row == 0)[None] & (lane < HALF)[None]
                sym[:, :, :LANES] = jnp.where(place, real - pltpu.roll(imag, HALF, 2), sym[:, :, :LANES])
                sym[:, :, LANES:] = jnp.where(place, imag + pltpu.roll(real, HALF, 2), sym[:, :, LANES:])

        back[chunk] = x_inverse(sym[...], (xi[0], xi[1]), xt)
        all_to_all(back, returned, chunk, BACK)

    def along_y(chunk):
        wait_for(returned.at[chunk], recv_sem.at[BACK, chunk])
        for index in (2 * chunk, 2 * chunk + 1):
            first = 16 * (index % 2)
            rows = returned[chunk, first : first + 16].reshape(LANES, LANES)
            width = 2 * LANES if index else 3 * LANES
            total = product(split(rows), (yi[0, :, :width], yi[1, :, :width]), ((0,), (0,)))
            lines[index, 0], lines[index, 1] = y_line(total, index, yt[0], yt[1])

    forward(0)

    @pl.when(special)
    def _():
        blocks = received[0]
        turned = pltpu.roll(pltpu.roll(blocks, HALF, 2), 4, 1)
        blocks = jnp.where((lane < HALF)[None], blocks, turned)
        along_x(jnp.where(upper(blocks.shape), blocks, 0.0), SPECIAL)

    forward(1)
    average(0)

    @pl.when(special)
    def _():
        average(SPECIAL)

    forward(2)
    average(1)
    forward(3)
    backward(0)
    average(2)
    backward(1)
    average(3)
    backward(2)
    backward(3)

    for chunk in range(CHUNKS):
        along_y(chunk)
    for index, value in enumerate(y_result([(lines[index, 0], lines[index, 1]) for index in range(8)])):
        out[:, index, :] = value

    for chunk in range(CHUNKS):
        for kind in (SEND, BACK):
            wait_for(received.at[chunk], send_sem.at[kind, chunk])
        for kind in (POWER, MEAN):
            wait_for(powers.at[chunk, pl.ds(0, PLANES - 1)], send_sem.at[kind, chunk])

    @pl.when(special)
    def _():
        for kind in (POWER, MEAN):
            wait_for(powers.at[SPECIAL, pl.ds(0, PLANES - 1)], send_sem.at[kind, SPECIAL])


def correct(error_field, x_shape, y_shape):
    shape = (OWN, 16, LANES)
    operands = [
        error_field.reshape(shape), y_forward_table(), y_inverse_table(), x_table(-1), x_table(1), y_twist(), x_twist(), *x_choices(),
        x_shape.reshape(16, LANES), y_shape,
    ]
    operands = [jnp.asarray(operand) for operand in operands]
    inside = [pltpu.VMEM(operand.shape, operand.dtype) for operand in operands]
    inside[-1] = pltpu.SMEM(y_shape.shape, F32)
    outside = pl.BlockSpec(memory_space=pltpu.HBM)
    done = pl.pallas_call(
        kernel,
        out_shape=pltpu.VMEM(shape, F32),
        in_specs=[outside] * len(operands),
        out_specs=pl.BlockSpec(memory_space=pltpu.VMEM),
        scratch_shapes=inside
        + [
            pltpu.VMEM((CHUNKS, FFT, 8, LANES), F32),
            pltpu.VMEM((CHUNKS, FFT, 8, LANES), F32),
            pltpu.VMEM((CHUNKS + 1, 16, 8, 2 * LANES), F32),
            pltpu.VMEM((CHUNKS + 1, PLANES, 8, LANES), F32),
            pltpu.VMEM((CHUNKS + 1, PLANES, 8, LANES), F32),
            pltpu.VMEM((CHUNKS + 1, PLANES, 8, LANES), F32),
            pltpu.VMEM((2, CHUNKS + 1, 16, 8, LANES), F32),
            pltpu.VMEM((CHUNKS, FFT, 8, LANES), F32),
            pltpu.VMEM((CHUNKS, FFT, 8, LANES), F32),
            pltpu.VMEM((16, 8, 2 * LANES), F32),
            pltpu.VMEM((8, 2, OWN, LANES), F32),
            pltpu.SemaphoreType.DMA((len(operands),)),
            pltpu.SemaphoreType.DMA((4, CHUNKS + 1)),
            pltpu.SemaphoreType.DMA((4, CHUNKS + 1)),
        ],
        compiler_params=pltpu.CompilerParams(
            collective_id=0, has_side_effects=True, vmem_limit_bytes=60 * 1024 * 1024
        ),
    )(*operands)
    return done.reshape(error_field.shape)


def solution(mesh):
    placed = (P("fft", "plane", None), P(), P())
    return jax.shard_map(
        correct, mesh=mesh, in_specs=placed, out_specs=P("fft", "plane", None), check_vma=False
    )
```

```python
import math

import jax
import jax.numpy as jnp
import ml_dtypes
import numpy as np
from jax import lax
from jax.experimental import pallas as pl
from jax.experimental.pallas import tpu as pltpu
from jax.sharding import PartitionSpec as P

F32 = jnp.float32
BF16 = jnp.bfloat16
N = 2048
FFT = 32
PLANES = 16
OWN = N // FFT
HALF = 64
LANES = 128
CHUNKS = 4
SPECIAL = CHUNKS
MESH = pl.DeviceIdType.MESH


def two_parts(table):
    table = np.asarray(table, np.float64)
    high = table.astype(np.float32).astype(ml_dtypes.bfloat16)
    low = (table - high.astype(np.float64)).astype(np.float32).astype(ml_dtypes.bfloat16)
    return np.stack([high, low])


def row_order():
    block, part, step = np.meshgrid(np.arange(16), np.arange(2), np.arange(4), indexing="ij")
    return part.reshape(-1), (block * 4 + step).reshape(-1)


def y_forward_table():
    part, row = row_order()
    angle = 2 * np.pi / LANES * (row[:, None] * np.arange(LANES)[None, :] % LANES)
    cosine, sine = np.cos(angle), np.sin(angle)
    part = part[:, None]
    table = np.concatenate([np.where(part == 0, cosine, -sine), np.where(part == 0, sine, cosine)], 1)
    extra = np.zeros((16, 2 * LANES))
    extra[0, :LANES] = 1 - 2 * (np.arange(LANES) % 2)
    return two_parts(np.concatenate([table, extra], 0))


def y_inverse_table():
    part, row = row_order()
    column = np.arange(LANES)
    angle = 2 * np.pi / LANES * (row[:, None] * column[None, :] % LANES)
    cosine, sine = np.cos(angle), np.sin(angle)
    part, row = part[:, None], row[:, None]
    plain = np.concatenate([np.where(part == 0, cosine, -sine), np.where(part == 0, sine, cosine)], 1)
    sign = (1 - 2 * (column % 2))[None, :]
    first = np.where(part == 0, np.where(row == 0, 1.0, 2 * cosine), np.where(row == 0, sign, -2 * sine))
    return two_parts(np.concatenate([plain, first], 1) / (N * N))


def x_table(direction):
    line = np.arange(HALF)
    angle = 2 * np.pi / HALF * (line[:, None] * line[None, :] % HALF)
    both = np.eye(2)
    cosine, sine = np.kron(both, np.cos(angle)), direction * np.kron(both, np.sin(angle))
    return two_parts(np.block([[cosine, sine], [-sine, cosine]]))


def y_twist():
    angle = 2 * np.pi / N * (np.arange(16)[:, None] * np.arange(LANES)[None, :] % N)
    return np.stack([np.cos(angle), np.sin(angle)]).astype(np.float32)


def x_twist():
    half = np.arange(8)[None, :, None] // 4
    line = np.arange(16)[:, None, None]
    column = np.arange(LANES)[None, None, :] % HALF
    inner = 2 * np.pi / FFT * (half * line % FFT) * np.ones_like(column)
    outer = 2 * np.pi / N * ((2 * line + half) * column % N)
    return np.stack([np.cos(inner), np.sin(inner), np.cos(outer), np.sin(outer)]).astype(np.float32)


def x_choices():
    pick, spread = np.zeros((2, 5, FFT, LANES)), np.zeros((2, 5, 16, LANES))
    for sign in range(2):
        for p in range(FFT):
            for q in range(HALF):
                kx = p + FFT * q if sign == 0 else (N - p - FFT * q) % N
                case = 4 if sign == 1 and p == 0 and q % 4 == 0 else q % 4
                pick[sign, case, p % 2 * 16 + p // 2, kx % LANES] = 1
                spread[sign, case, kx // LANES, [q, HALF + q]] = 1
    return pick.reshape(2 * 5 * FFT, LANES).astype(ml_dtypes.bfloat16), spread.astype(ml_dtypes.bfloat16)


def split(values):
    high = values.astype(BF16)
    return high, (values - high.astype(F32)).astype(BF16)


def dot(left, right, dims):
    return lax.dot_general(left, right, (dims, ((), ())), preferred_element_type=F32)


def product(left, right, dims):
    (left_high, left_low), (right_high, right_low) = left, right
    return dot(left_high, right_high, dims) + (dot(left_low, right_high, dims) + dot(left_high, right_low, dims))


def turn(value, part, whole, direction):
    real, imag = value
    part = part % whole
    eighth = 8 * part
    if eighth % whole == 0:
        eighth = eighth // whole
        root = math.sqrt(0.5)
        if eighth == 0:
            return value
        if eighth == 4:
            return (-real, -imag)
        if eighth == 2 or eighth == 6:
            return (-imag, real) if (eighth == 2) == (direction > 0) else (imag, -real)
    cosine, sine = math.cos(2 * math.pi * part / whole), direction * math.sin(2 * math.pi * part / whole)
    return (real * cosine - imag * sine, real * sine + imag * cosine)


def plus(left, right):
    return (left[0] + right[0], left[1] + right[1])


def minus(left, right):
    return (left[0] - right[0], left[1] - right[1])


def small_dft(values, direction):
    size = len(values)
    if size == 1:
        return values
    even = small_dft(values[0::2], direction)
    odd = small_dft(values[1::2], direction)
    odd = [turn(odd[index], index, size, direction) for index in range(size // 2)]
    return [plus(even[index], odd[index]) for index in range(size // 2)] + [
        minus(even[index], odd[index]) for index in range(size // 2)
    ]


def dft16(real, imag, direction):
    shape = (4, 4) + real.shape[1:]
    real, imag = real.reshape(shape), imag.reshape(shape)
    first = small_dft([(real[u], imag[u]) for u in range(4)], direction)
    second = []
    for v in range(4):
        turned = [turn((first[w][0][v], first[w][1][v]), w * v, 16, direction) for w in range(4)]
        second.append((jnp.stack([value[0] for value in turned]), jnp.stack([value[1] for value in turned])))
    done = small_dft(second, direction)
    flat = (16,) + real.shape[2:]
    return (
        jnp.stack([value[0] for value in done]).reshape(flat),
        jnp.stack([value[1] for value in done]).reshape(flat),
    )


def real_dft(values):
    size = len(values)
    if size == 2:
        return [values[0] + values[1], values[0] - values[1]]
    even, odd = real_dft(values[0::2]), real_dft(values[1::2])
    half, quarter = size // 2, size // 4
    out = [None] * (half + 1)
    out[0], out[half] = even[0] + odd[0], even[0] - odd[0]
    out[quarter] = (even[quarter], -odd[quarter])
    for index in range(1, quarter):
        turned = turn(odd[index], index, size, -1)
        out[index] = plus(even[index], turned)
        back = minus(even[index], turned)
        out[half - index] = (back[0], -back[1])
    return out


def real_inverse(values):
    half = len(values) - 1
    size = 2 * half
    if size == 2:
        return [values[0] + values[1], values[0] - values[1]]
    quarter = size // 4
    even, odd = [None] * (quarter + 1), [None] * (quarter + 1)
    even[0], odd[0] = values[0] + values[half], values[0] - values[half]
    even[quarter], odd[quarter] = 2.0 * values[quarter][0], -2.0 * values[quarter][1]
    for index in range(1, quarter):
        mirror = (values[half - index][0], -values[half - index][1])
        even[index] = plus(values[index], mirror)
        odd[index] = turn(minus(values[index], mirror), index, size, 1)
    out = [None] * size
    out[0::2], out[1::2] = real_inverse(even), real_inverse(odd)
    return out


def y_operands(field, twist_cos, twist_sin):
    parts = real_dft(field)
    sign = 1.0 - 2.0 * (lax.broadcasted_iota(jnp.int32, (OWN, LANES), 1) % 2).astype(F32)

    def twisted(index):
        cosine, sine = twist_cos[index][None, :], twist_sin[index][None, :]
        if index == 8:
            return jnp.concatenate([parts[8] * cosine, -parts[8] * sine], 1)
        real, imag = parts[index]
        return jnp.concatenate([real * cosine + imag * sine, imag * cosine - real * sine], 1)

    signs = jnp.concatenate([sign, sign], 1)
    out = [jnp.concatenate([jnp.concatenate([parts[0], jnp.zeros_like(parts[0])], 1), twisted(8)], 0)]
    for index in range(1, 8):
        value = twisted(index)
        out.append(jnp.concatenate([value, value * signs], 0))
    return out


def y_line(total, index, twist_cos, twist_sin):
    if index == 0:
        real, imag = total[OWN:, :LANES], total[OWN:, LANES : 2 * LANES]
        return total[:OWN, 2 * LANES :], 2.0 * (real * twist_cos[8][None, :] - imag * twist_sin[8][None, :])
    sign = 1.0 - 2.0 * (lax.broadcasted_iota(jnp.int32, (OWN, LANES), 1) % 2).astype(F32)
    real = total[:OWN, :LANES] + sign * total[OWN:, :LANES]
    imag = total[:OWN, LANES:] + sign * total[OWN:, LANES:]
    cosine, sine = twist_cos[index][None, :], twist_sin[index][None, :]
    return real * cosine - imag * sine, real * sine + imag * cosine


def y_result(lines):
    values = real_inverse([lines[0][0], *lines[1:], lines[0][1]])
    return [jnp.clip(value, -1.0, 1.0) for value in values]


def upper(shape):
    return lax.broadcasted_iota(jnp.int32, shape, 1) < 4


def x_forward(blocks, table, twist):
    total, rest = blocks[:16] + blocks[16:], blocks[:16] - blocks[16:]
    top = upper(total.shape)
    real = jnp.where(top, total, pltpu.roll(rest, 4, 1))
    imag = jnp.where(top, pltpu.roll(total, 4, 1), rest)
    real, imag = real * twist[0] + imag * twist[1], imag * twist[0] - real * twist[1]
    real, imag = dft16(real, imag, -1)
    both = jnp.concatenate([real * twist[2] + imag * twist[3], imag * twist[2] - real * twist[3]], 2)
    return product(split(both.reshape(LANES, 2 * LANES)), table, ((1,), (0,))).reshape(16, 8, 2 * LANES)


def x_inverse(values, table, twist):
    out = product(split(values.reshape(LANES, 2 * LANES)), table, ((1,), (0,))).reshape(16, 8, 2 * LANES)
    real, imag = out[:, :, :LANES], out[:, :, LANES:]
    real, imag = dft16(real * twist[2] - imag * twist[3], real * twist[3] + imag * twist[2], 1)
    real, imag = real * twist[0] - imag * twist[1], real * twist[1] + imag * twist[0]
    top = upper(real.shape)
    even = jnp.where(top, real, pltpu.roll(imag, 4, 1))
    odd = jnp.where(top, pltpu.roll(real, 4, 1), imag)
    return jnp.concatenate([even + odd, even - odd], 0)


def x_factors(shape, pick, spread):
    rest, parts = shape, []
    for _ in range(3):
        part = rest.astype(BF16)
        parts.append(part)
        rest = rest - part.astype(F32)
    chosen = [dot(pick, part, ((1,), (1,))).astype(BF16) for part in parts]
    out = []
    for sign in range(2):
        total = None
        for part in reversed(chosen):
            for case in range(4 + sign):
                start = FFT * (5 * sign + case)
                value = dot(part[start : start + FFT], spread[sign, case], ((1,), (0,)))
                total = value if total is None else total + value
        even, odd = total[:16, None, :], total[16:, None, :]
        out.append(jnp.where(upper((16, 8, LANES)), even, odd))
    return out


SEND, POWER, MEAN, BACK = range(4)


def far_first(step):
    return lax.rem(12 + (step + 1) // 2 * (1 - 2 * lax.rem(step, 2)), 8)


def kernel(
    field_hbm, yf_hbm, yi_hbm, xf_hbm, xi_hbm, yt_hbm, xt_hbm, pick_hbm, spread_hbm, xs_hbm, ys_hbm,
    out,
    field, yf, yi, xf, xi, yt, xt, pick, spread, xs, y_shape,
    sent, received, spec, power, powers, root, bound, back, returned, sym, lines,
    load_sem, send_sem, recv_sem,
):
    me = lax.axis_index("fft")
    plane = lax.axis_index("plane")
    other = plane + 1 - 2 * lax.rem(plane, 2)
    special = me == 0
    barrier = pltpu.get_barrier_semaphore()

    def fft_peer(step):
        part = step // 8
        place = 2 * lax.rem(lax.rem(me, 4) // 2 + 1 + part, 2) + part // 2
        return lax.rem(me // 4 + far_first(lax.rem(step, 8)), 8) * 4 + place

    def plane_peer(step):
        return lax.rem(plane // 2 + far_first(step // 2), 8) * 2 + lax.rem(plane + 1 + step, 2)

    loads = []
    for index, (source, target) in enumerate(
        [
            (field_hbm, field), (yt_hbm, yt), (yf_hbm, yf), (ys_hbm, y_shape), (xs_hbm, xs), (pick_hbm, pick),
            (spread_hbm, spread), (xf_hbm, xf), (xt_hbm, xt), (xi_hbm, xi), (yi_hbm, yi),
        ]
    ):
        loads.append(pltpu.make_async_copy(source, target, load_sem.at[index]))
    for copy in loads[:3]:
        copy.start()

    line, place = me // 4, lax.rem(me, 4)
    ring, side = plane // 2, lax.rem(plane, 2)
    partners = [
        (min(along, 8 - along) + 1, lax.rem(line + along, 8) * 4 + lax.rem(place + turn_by, 4), other)
        for along in range(8)
        for turn_by in range(4)
    ] + [
        (min(along, 8 - along) + across, me, lax.rem(ring + along, 8) * 2 + lax.rem(side + across, 2))
        for along in range(8)
        for across in range(2)
        if along + across
    ]
    for _, fft_index, plane_index in sorted(partners, key=lambda partner: -partner[0]):
        pl.semaphore_signal(barrier, inc=1, device_id=(fft_index, plane_index), device_id_type=MESH)

    for copy in loads[3:]:
        copy.start()

    def all_to_all(source, target, chunk, kind):
        @pl.loop(0, FFT)
        def _(step):
            peer = fft_peer(step)
            pltpu.make_async_remote_copy(
                src_ref=source.at[chunk, peer],
                dst_ref=target.at[chunk, me],
                send_sem=send_sem.at[kind, chunk],
                recv_sem=recv_sem.at[kind, chunk],
                device_id=(peer, other),
                device_id_type=MESH,
            ).start()

    def to_planes(source, target, chunk, kind):
        @pl.loop(0, PLANES - 1)
        def _(step):
            peer = plane_peer(step)
            pltpu.make_async_remote_copy(
                src_ref=source(peer),
                dst_ref=target,
                send_sem=send_sem.at[kind, chunk],
                recv_sem=recv_sem.at[kind, chunk],
                device_id=(me, peer),
                device_id_type=MESH,
            ).start()

    def wait_for(ref, sem):
        pltpu.make_async_copy(ref, ref, sem).wait()

    for copy in loads[:3]:
        copy.wait()
    operands = y_operands([field[:, index, :] for index in range(16)], yt[0], yt[1])
    for index, operand in enumerate(operands):
        operand = split(operand)
        done = product((yf[0, :128], yf[1, :128]), operand, ((1,), (1,)))
        if index == 0:
            extra = product((yf[0, 128:], yf[1, 128:]), operand, ((1,), (1,)))[0:1, :]
            row = lax.broadcasted_iota(jnp.int32, (128, LANES), 0)
            lane = lax.broadcasted_iota(jnp.int32, (128, LANES), 1)
            done = jnp.where((row == 4) & (lane < HALF), extra, done)
        first = 16 * (index % 2)
        sent[index // 2, first : first + 16] = done.reshape(16, 8, LANES)
        if index == 1:
            pl.semaphore_wait(barrier, FFT + PLANES - 1)
        if index % 2 == 1:
            all_to_all(sent, received, index // 2, SEND)

    for copy in loads[3:]:
        copy.wait()
    row = lax.broadcasted_iota(jnp.int32, (8, LANES), 0) % 4
    lane = lax.broadcasted_iota(jnp.int32, (8, LANES), 1)
    x_here, x_other = x_factors(xs[...], pick[...], spread[...])
    for chunk in range(CHUNKS):
        here, opposite = jnp.zeros((8, LANES), F32), jnp.zeros((8, LANES), F32)
        group = 2 * chunk + me // 16
        for half in range(2):
            for step in range(4):
                line = 4 * lax.rem(me, 16) + step
                ky = jnp.where(group == 0, 8 * half + 16 * line, group + 16 * (line + 64 * half))
                place = (row == step) & (lane // HALF == half)
                here = jnp.where(place, y_shape[ky], here)
                opposite = jnp.where(place, y_shape[lax.rem(N - ky, N)], opposite)
        bound[0, chunk] = here[None] * x_here
        bound[1, chunk] = opposite[None] * x_other

    @pl.when(special)
    def _():
        here = jnp.where(lane < HALF, y_shape[0], y_shape[N // 2])
        bound[0, SPECIAL] = here[None] * x_here
        bound[1, SPECIAL] = here[None] * x_other

    def along_x(blocks, chunk):
        done = x_forward(blocks, (xf[0], xf[1]), xt)
        spec[chunk] = done
        real, imag = done[:, :, :LANES], done[:, :, LANES:]
        power[chunk] = real * real + imag * imag
        powers[chunk, plane] = power[chunk, plane]
        to_planes(lambda peer: power.at[chunk, peer], powers.at[chunk, plane], chunk, POWER)

    def forward(chunk):
        wait_for(received.at[chunk], recv_sem.at[SEND, chunk])
        along_x(received[chunk], chunk)

    def average(chunk):
        wait_for(powers.at[chunk, pl.ds(0, PLANES - 1)], recv_sem.at[POWER, chunk])
        total = powers[chunk, 0]
        for index in range(1, PLANES):
            total = total + powers[chunk, index]
        root[chunk, plane] = jnp.sqrt(total * (1.0 / PLANES))
        to_planes(lambda peer: root.at[chunk, plane], root.at[chunk, plane], chunk, MEAN)

    def clipped(chunk):
        wait_for(root.at[chunk, pl.ds(0, PLANES - 1)], recv_sem.at[MEAN, chunk])
        here, opposite = bound[0, chunk] * root[chunk], bound[1, chunk] * root[chunk]
        real, imag = spec[chunk, :, :, :LANES], spec[chunk, :, :, LANES:]
        return [
            0.5 * (jnp.clip(value, -here, here) + jnp.clip(value, -opposite, opposite)) for value in (real, imag)
        ]

    def backward(chunk):
        real, imag = clipped(chunk)
        sym[:, :, :LANES] = real
        sym[:, :, LANES:] = imag
        if chunk == 0:

            @pl.when(special)
            def _():
                real, imag = clipped(SPECIAL)
                place = (row == 0)[None] & (lane < HALF)[None]
                sym[:, :, :LANES] = jnp.where(place, real - pltpu.roll(imag, HALF, 2), sym[:, :, :LANES])
                sym[:, :, LANES:] = jnp.where(place, imag + pltpu.roll(real, HALF, 2), sym[:, :, LANES:])

        back[chunk] = x_inverse(sym[...], (xi[0], xi[1]), xt)
        all_to_all(back, returned, chunk, BACK)

    def along_y(chunk):
        wait_for(returned.at[chunk], recv_sem.at[BACK, chunk])
        for index in (2 * chunk, 2 * chunk + 1):
            first = 16 * (index % 2)
            rows = returned[chunk, first : first + 16].reshape(LANES, LANES)
            width = 2 * LANES if index else 3 * LANES
            total = product(split(rows), (yi[0, :, :width], yi[1, :, :width]), ((0,), (0,)))
            lines[index, 0], lines[index, 1] = y_line(total, index, yt[0], yt[1])

    forward(0)

    @pl.when(special)
    def _():
        blocks = received[0]
        turned = pltpu.roll(pltpu.roll(blocks, HALF, 2), 4, 1)
        blocks = jnp.where((lane < HALF)[None], blocks, turned)
        along_x(jnp.where(upper(blocks.shape), blocks, 0.0), SPECIAL)

    forward(1)
    average(0)

    @pl.when(special)
    def _():
        average(SPECIAL)

    forward(2)
    forward(3)
    average(1)
    average(2)
    backward(0)
    average(3)
    backward(1)
    backward(2)
    backward(3)

    for chunk in range(CHUNKS):
        along_y(chunk)
    for index, value in enumerate(y_result([(lines[index, 0], lines[index, 1]) for index in range(8)])):
        out[:, index, :] = value

    for chunk in range(CHUNKS):
        for kind in (SEND, BACK):
            wait_for(received.at[chunk], send_sem.at[kind, chunk])
        for kind in (POWER, MEAN):
            wait_for(powers.at[chunk, pl.ds(0, PLANES - 1)], send_sem.at[kind, chunk])

    @pl.when(special)
    def _():
        for kind in (POWER, MEAN):
            wait_for(powers.at[SPECIAL, pl.ds(0, PLANES - 1)], send_sem.at[kind, SPECIAL])


def correct(error_field, x_shape, y_shape):
    shape = (OWN, 16, LANES)
    operands = [
        error_field.reshape(shape), y_forward_table(), y_inverse_table(), x_table(-1), x_table(1), y_twist(), x_twist(), *x_choices(),
        x_shape.reshape(16, LANES), y_shape,
    ]
    operands = [jnp.asarray(operand) for operand in operands]
    inside = [pltpu.VMEM(operand.shape, operand.dtype) for operand in operands]
    inside[-1] = pltpu.SMEM(y_shape.shape, F32)
    outside = pl.BlockSpec(memory_space=pltpu.HBM)
    done = pl.pallas_call(
        kernel,
        out_shape=pltpu.VMEM(shape, F32),
        in_specs=[outside] * len(operands),
        out_specs=pl.BlockSpec(memory_space=pltpu.VMEM),
        scratch_shapes=inside
        + [
            pltpu.VMEM((CHUNKS, FFT, 8, LANES), F32),
            pltpu.VMEM((CHUNKS, FFT, 8, LANES), F32),
            pltpu.VMEM((CHUNKS + 1, 16, 8, 2 * LANES), F32),
            pltpu.VMEM((CHUNKS + 1, PLANES, 8, LANES), F32),
            pltpu.VMEM((CHUNKS + 1, PLANES, 8, LANES), F32),
            pltpu.VMEM((CHUNKS + 1, PLANES, 8, LANES), F32),
            pltpu.VMEM((2, CHUNKS + 1, 16, 8, LANES), F32),
            pltpu.VMEM((CHUNKS, FFT, 8, LANES), F32),
            pltpu.VMEM((CHUNKS, FFT, 8, LANES), F32),
            pltpu.VMEM((16, 8, 2 * LANES), F32),
            pltpu.VMEM((8, 2, OWN, LANES), F32),
            pltpu.SemaphoreType.DMA((len(operands),)),
            pltpu.SemaphoreType.DMA((4, CHUNKS + 1)),
            pltpu.SemaphoreType.DMA((4, CHUNKS + 1)),
        ],
        compiler_params=pltpu.CompilerParams(
            collective_id=0, has_side_effects=True, vmem_limit_bytes=60 * 1024 * 1024
        ),
    )(*operands)
    return done.reshape(error_field.shape)


def solution(mesh):
    placed = (P("fft", "plane", None), P(), P())
    return jax.shard_map(
        correct, mesh=mesh, in_specs=placed, out_specs=P("fft", "plane", None), check_vma=False
    )
```

```python
import math

import jax
import jax.numpy as jnp
import ml_dtypes
import numpy as np
from jax import lax
from jax.experimental import pallas as pl
from jax.experimental.pallas import tpu as pltpu
from jax.sharding import PartitionSpec as P

F32 = jnp.float32
BF16 = jnp.bfloat16
N = 2048
FFT = 32
PLANES = 16
OWN = N // FFT
HALF = 64
LANES = 128
CHUNKS = 4
SPECIAL = CHUNKS
MESH = pl.DeviceIdType.MESH


def two_parts(table):
    table = np.asarray(table, np.float64)
    high = table.astype(np.float32).astype(ml_dtypes.bfloat16)
    low = (table - high.astype(np.float64)).astype(np.float32).astype(ml_dtypes.bfloat16)
    return np.stack([high, low])


def row_order():
    block, part, step = np.meshgrid(np.arange(16), np.arange(2), np.arange(4), indexing="ij")
    return part.reshape(-1), (block * 4 + step).reshape(-1)


def y_forward_table():
    part, row = row_order()
    angle = 2 * np.pi / LANES * (row[:, None] * np.arange(LANES)[None, :] % LANES)
    cosine, sine = np.cos(angle), np.sin(angle)
    part = part[:, None]
    table = np.concatenate([np.where(part == 0, cosine, -sine), np.where(part == 0, sine, cosine)], 1)
    extra = np.zeros((16, 2 * LANES))
    extra[0, :LANES] = 1 - 2 * (np.arange(LANES) % 2)
    return two_parts(np.concatenate([table, extra], 0))


def y_inverse_table():
    part, row = row_order()
    column = np.arange(LANES)
    angle = 2 * np.pi / LANES * (row[:, None] * column[None, :] % LANES)
    cosine, sine = np.cos(angle), np.sin(angle)
    part, row = part[:, None], row[:, None]
    plain = np.concatenate([np.where(part == 0, cosine, -sine), np.where(part == 0, sine, cosine)], 1)
    sign = (1 - 2 * (column % 2))[None, :]
    first = np.where(part == 0, np.where(row == 0, 1.0, 2 * cosine), np.where(row == 0, sign, -2 * sine))
    return two_parts(np.concatenate([plain, first], 1) / (N * N))


def x_table(direction):
    line = np.arange(HALF)
    angle = 2 * np.pi / HALF * (line[:, None] * line[None, :] % HALF)
    both = np.eye(2)
    cosine, sine = np.kron(both, np.cos(angle)), direction * np.kron(both, np.sin(angle))
    return two_parts(np.block([[cosine, sine], [-sine, cosine]]))


def y_twist():
    angle = 2 * np.pi / N * (np.arange(16)[:, None] * np.arange(LANES)[None, :] % N)
    return np.stack([np.cos(angle), np.sin(angle)]).astype(np.float32)


def x_twist():
    half = np.arange(8)[None, :, None] // 4
    line = np.arange(16)[:, None, None]
    column = np.arange(LANES)[None, None, :] % HALF
    inner = 2 * np.pi / FFT * (half * line % FFT) * np.ones_like(column)
    outer = 2 * np.pi / N * ((2 * line + half) * column % N)
    return np.stack([np.cos(inner), np.sin(inner), np.cos(outer), np.sin(outer)]).astype(np.float32)


def x_choices():
    pick, spread = np.zeros((2, 5, FFT, LANES)), np.zeros((2, 5, 16, LANES))
    for sign in range(2):
        for p in range(FFT):
            for q in range(HALF):
                kx = p + FFT * q if sign == 0 else (N - p - FFT * q) % N
                case = 4 if sign == 1 and p == 0 and q % 4 == 0 else q % 4
                pick[sign, case, p % 2 * 16 + p // 2, kx % LANES] = 1
                spread[sign, case, kx // LANES, [q, HALF + q]] = 1
    return pick.reshape(2 * 5 * FFT, LANES).astype(ml_dtypes.bfloat16), spread.astype(ml_dtypes.bfloat16)


def split(values):
    high = values.astype(BF16)
    return high, (values - high.astype(F32)).astype(BF16)


def dot(left, right, dims):
    return lax.dot_general(left, right, (dims, ((), ())), preferred_element_type=F32)


def product(left, right, dims):
    (left_high, left_low), (right_high, right_low) = left, right
    return dot(left_high, right_high, dims) + (dot(left_low, right_high, dims) + dot(left_high, right_low, dims))


def turn(value, part, whole, direction):
    real, imag = value
    part = part % whole
    eighth = 8 * part
    if eighth % whole == 0:
        eighth = eighth // whole
        root = math.sqrt(0.5)
        if eighth == 0:
            return value
        if eighth == 4:
            return (-real, -imag)
        if eighth == 2 or eighth == 6:
            return (-imag, real) if (eighth == 2) == (direction > 0) else (imag, -real)
    cosine, sine = math.cos(2 * math.pi * part / whole), direction * math.sin(2 * math.pi * part / whole)
    return (real * cosine - imag * sine, real * sine + imag * cosine)


def plus(left, right):
    return (left[0] + right[0], left[1] + right[1])


def minus(left, right):
    return (left[0] - right[0], left[1] - right[1])


def small_dft(values, direction):
    size = len(values)
    if size == 1:
        return values
    even = small_dft(values[0::2], direction)
    odd = small_dft(values[1::2], direction)
    odd = [turn(odd[index], index, size, direction) for index in range(size // 2)]
    return [plus(even[index], odd[index]) for index in range(size // 2)] + [
        minus(even[index], odd[index]) for index in range(size // 2)
    ]


def dft16(real, imag, direction):
    shape = (4, 4) + real.shape[1:]
    real, imag = real.reshape(shape), imag.reshape(shape)
    first = small_dft([(real[u], imag[u]) for u in range(4)], direction)
    second = []
    for v in range(4):
        turned = [turn((first[w][0][v], first[w][1][v]), w * v, 16, direction) for w in range(4)]
        second.append((jnp.stack([value[0] for value in turned]), jnp.stack([value[1] for value in turned])))
    done = small_dft(second, direction)
    flat = (16,) + real.shape[2:]
    return (
        jnp.stack([value[0] for value in done]).reshape(flat),
        jnp.stack([value[1] for value in done]).reshape(flat),
    )


def real_dft(values):
    size = len(values)
    if size == 2:
        return [values[0] + values[1], values[0] - values[1]]
    even, odd = real_dft(values[0::2]), real_dft(values[1::2])
    half, quarter = size // 2, size // 4
    out = [None] * (half + 1)
    out[0], out[half] = even[0] + odd[0], even[0] - odd[0]
    out[quarter] = (even[quarter], -odd[quarter])
    for index in range(1, quarter):
        turned = turn(odd[index], index, size, -1)
        out[index] = plus(even[index], turned)
        back = minus(even[index], turned)
        out[half - index] = (back[0], -back[1])
    return out


def real_inverse(values):
    half = len(values) - 1
    size = 2 * half
    if size == 2:
        return [values[0] + values[1], values[0] - values[1]]
    quarter = size // 4
    even, odd = [None] * (quarter + 1), [None] * (quarter + 1)
    even[0], odd[0] = values[0] + values[half], values[0] - values[half]
    even[quarter], odd[quarter] = 2.0 * values[quarter][0], -2.0 * values[quarter][1]
    for index in range(1, quarter):
        mirror = (values[half - index][0], -values[half - index][1])
        even[index] = plus(values[index], mirror)
        odd[index] = turn(minus(values[index], mirror), index, size, 1)
    out = [None] * size
    out[0::2], out[1::2] = real_inverse(even), real_inverse(odd)
    return out


def y_operands(field, twist_cos, twist_sin):
    parts = real_dft(field)
    sign = 1.0 - 2.0 * (lax.broadcasted_iota(jnp.int32, (OWN, LANES), 1) % 2).astype(F32)

    def twisted(index):
        cosine, sine = twist_cos[index][None, :], twist_sin[index][None, :]
        if index == 8:
            return jnp.concatenate([parts[8] * cosine, -parts[8] * sine], 1)
        real, imag = parts[index]
        return jnp.concatenate([real * cosine + imag * sine, imag * cosine - real * sine], 1)

    signs = jnp.concatenate([sign, sign], 1)
    out = [jnp.concatenate([jnp.concatenate([parts[0], jnp.zeros_like(parts[0])], 1), twisted(8)], 0)]
    for index in range(1, 8):
        value = twisted(index)
        out.append(jnp.concatenate([value, value * signs], 0))
    return out


def y_line(total, index, twist_cos, twist_sin):
    if index == 0:
        real, imag = total[OWN:, :LANES], total[OWN:, LANES : 2 * LANES]
        return total[:OWN, 2 * LANES :], 2.0 * (real * twist_cos[8][None, :] - imag * twist_sin[8][None, :])
    sign = 1.0 - 2.0 * (lax.broadcasted_iota(jnp.int32, (OWN, LANES), 1) % 2).astype(F32)
    real = total[:OWN, :LANES] + sign * total[OWN:, :LANES]
    imag = total[:OWN, LANES:] + sign * total[OWN:, LANES:]
    cosine, sine = twist_cos[index][None, :], twist_sin[index][None, :]
    return real * cosine - imag * sine, real * sine + imag * cosine


def y_result(lines):
    values = real_inverse([lines[0][0], *lines[1:], lines[0][1]])
    return [jnp.clip(value, -1.0, 1.0) for value in values]


def upper(shape):
    return lax.broadcasted_iota(jnp.int32, shape, 1) < 4


def x_forward(blocks, table, twist):
    total, rest = blocks[:16] + blocks[16:], blocks[:16] - blocks[16:]
    top = upper(total.shape)
    real = jnp.where(top, total, pltpu.roll(rest, 4, 1))
    imag = jnp.where(top, pltpu.roll(total, 4, 1), rest)
    real, imag = real * twist[0] + imag * twist[1], imag * twist[0] - real * twist[1]
    real, imag = dft16(real, imag, -1)
    both = jnp.concatenate([real * twist[2] + imag * twist[3], imag * twist[2] - real * twist[3]], 2)
    return product(split(both.reshape(LANES, 2 * LANES)), table, ((1,), (0,))).reshape(16, 8, 2 * LANES)


def x_inverse(values, table, twist):
    out = product(split(values.reshape(LANES, 2 * LANES)), table, ((1,), (0,))).reshape(16, 8, 2 * LANES)
    real, imag = out[:, :, :LANES], out[:, :, LANES:]
    real, imag = dft16(real * twist[2] - imag * twist[3], real * twist[3] + imag * twist[2], 1)
    real, imag = real * twist[0] - imag * twist[1], real * twist[1] + imag * twist[0]
    top = upper(real.shape)
    even = jnp.where(top, real, pltpu.roll(imag, 4, 1))
    odd = jnp.where(top, pltpu.roll(real, 4, 1), imag)
    return jnp.concatenate([even + odd, even - odd], 0)


def x_factors(shape, pick, spread):
    rest, parts = shape, []
    for _ in range(3):
        part = rest.astype(BF16)
        parts.append(part)
        rest = rest - part.astype(F32)
    chosen = [dot(pick, part, ((1,), (1,))).astype(BF16) for part in parts]
    out = []
    for sign in range(2):
        total = None
        for part in reversed(chosen):
            for case in range(4 + sign):
                start = FFT * (5 * sign + case)
                value = dot(part[start : start + FFT], spread[sign, case], ((1,), (0,)))
                total = value if total is None else total + value
        even, odd = total[:16, None, :], total[16:, None, :]
        out.append(jnp.where(upper((16, 8, LANES)), even, odd))
    return out


SEND, POWER, MEAN, BACK = range(4)


def far_first(step):
    return lax.rem(12 + (step + 1) // 2 * (1 - 2 * lax.rem(step, 2)), 8)


def kernel(
    field_hbm, yf_hbm, yi_hbm, xf_hbm, xi_hbm, yt_hbm, xt_hbm, pick_hbm, spread_hbm, xs_hbm, ys_hbm,
    out,
    field, yf, yi, xf, xi, yt, xt, pick, spread, xs, y_shape,
    sent, received, spec, power, powers, root, bound, back, returned, sym, lines,
    load_sem, send_sem, recv_sem,
):
    me = lax.axis_index("fft")
    plane = lax.axis_index("plane")
    other = plane + 1 - 2 * lax.rem(plane, 2)
    special = me == 0
    barrier = pltpu.get_barrier_semaphore()

    def fft_peer(step):
        part = step // 8
        place = 2 * lax.rem(lax.rem(me, 4) // 2 + 1 + part, 2) + part // 2
        return lax.rem(me // 4 + far_first(lax.rem(step, 8)), 8) * 4 + place

    def plane_peer(step):
        return lax.rem(plane // 2 + far_first(step // 2), 8) * 2 + lax.rem(plane + 1 + step, 2)

    loads = []
    for index, (source, target) in enumerate(
        [
            (field_hbm, field), (yt_hbm, yt), (yf_hbm, yf), (ys_hbm, y_shape), (xs_hbm, xs), (pick_hbm, pick),
            (spread_hbm, spread), (xf_hbm, xf), (xt_hbm, xt), (xi_hbm, xi), (yi_hbm, yi),
        ]
    ):
        loads.append(pltpu.make_async_copy(source, target, load_sem.at[index]))
    for copy in loads[:3]:
        copy.start()

    line, place = me // 4, lax.rem(me, 4)
    ring, side = plane // 2, lax.rem(plane, 2)
    partners = [
        (min(along, 8 - along) + 1, lax.rem(line + along, 8) * 4 + lax.rem(place + turn_by, 4), other)
        for along in range(8)
        for turn_by in range(4)
    ] + [
        (min(along, 8 - along) + across, me, lax.rem(ring + along, 8) * 2 + lax.rem(side + across, 2))
        for along in range(8)
        for across in range(2)
        if along + across
    ]
    for _, fft_index, plane_index in sorted(partners, key=lambda partner: -partner[0]):
        pl.semaphore_signal(barrier, inc=1, device_id=(fft_index, plane_index), device_id_type=MESH)

    for copy in loads[3:]:
        copy.start()

    def all_to_all(source, target, chunk, kind):
        @pl.loop(0, FFT)
        def _(step):
            peer = fft_peer(step)
            pltpu.make_async_remote_copy(
                src_ref=source.at[chunk, peer],
                dst_ref=target.at[chunk, me],
                send_sem=send_sem.at[kind, chunk],
                recv_sem=recv_sem.at[kind, chunk],
                device_id=(peer, other),
                device_id_type=MESH,
            ).start()

    def to_planes(source, target, chunk, kind):
        @pl.loop(0, PLANES - 1)
        def _(step):
            peer = plane_peer(step)
            pltpu.make_async_remote_copy(
                src_ref=source(peer),
                dst_ref=target,
                send_sem=send_sem.at[kind, chunk],
                recv_sem=recv_sem.at[kind, chunk],
                device_id=(me, peer),
                device_id_type=MESH,
            ).start()

    def wait_for(ref, sem):
        pltpu.make_async_copy(ref, ref, sem).wait()

    for copy in loads[:3]:
        copy.wait()
    operands = y_operands([field[:, index, :] for index in range(16)], yt[0], yt[1])
    for index, operand in enumerate(operands):
        operand = split(operand)
        done = product((yf[0, :128], yf[1, :128]), operand, ((1,), (1,)))
        if index == 0:
            extra = product((yf[0, 128:], yf[1, 128:]), operand, ((1,), (1,)))[0:1, :]
            row = lax.broadcasted_iota(jnp.int32, (128, LANES), 0)
            lane = lax.broadcasted_iota(jnp.int32, (128, LANES), 1)
            done = jnp.where((row == 4) & (lane < HALF), extra, done)
        first = 16 * (index % 2)
        sent[index // 2, first : first + 16] = done.reshape(16, 8, LANES)
        if index == 1:
            pl.semaphore_wait(barrier, FFT + PLANES - 1)
        if index % 2 == 1:
            all_to_all(sent, received, index // 2, SEND)

    for copy in loads[3:]:
        copy.wait()
    row = lax.broadcasted_iota(jnp.int32, (8, LANES), 0) % 4
    lane = lax.broadcasted_iota(jnp.int32, (8, LANES), 1)
    x_here, x_other = x_factors(xs[...], pick[...], spread[...])
    for chunk in range(CHUNKS):
        here, opposite = jnp.zeros((8, LANES), F32), jnp.zeros((8, LANES), F32)
        group = 2 * chunk + me // 16
        for half in range(2):
            for step in range(4):
                line = 4 * lax.rem(me, 16) + step
                ky = jnp.where(group == 0, 8 * half + 16 * line, group + 16 * (line + 64 * half))
                place = (row == step) & (lane // HALF == half)
                here = jnp.where(place, y_shape[ky], here)
                opposite = jnp.where(place, y_shape[lax.rem(N - ky, N)], opposite)
        bound[0, chunk] = here[None] * x_here
        bound[1, chunk] = opposite[None] * x_other

    @pl.when(special)
    def _():
        here = jnp.where(lane < HALF, y_shape[0], y_shape[N // 2])
        bound[0, SPECIAL] = here[None] * x_here
        bound[1, SPECIAL] = here[None] * x_other

    def along_x(blocks, chunk):
        done = x_forward(blocks, (xf[0], xf[1]), xt)
        spec[chunk] = done
        real, imag = done[:, :, :LANES], done[:, :, LANES:]
        power[chunk] = real * real + imag * imag
        powers[chunk, plane] = power[chunk, plane]
        to_planes(lambda peer: power.at[chunk, peer], powers.at[chunk, plane], chunk, POWER)

    def forward(chunk):
        wait_for(received.at[chunk], recv_sem.at[SEND, chunk])
        along_x(received[chunk], chunk)

    def average(chunk):
        wait_for(powers.at[chunk, pl.ds(0, PLANES - 1)], recv_sem.at[POWER, chunk])
        total = powers[chunk, 0]
        for index in range(1, PLANES):
            total = total + powers[chunk, index]
        root[chunk, plane] = jnp.sqrt(total * (1.0 / PLANES))
        to_planes(lambda peer: root.at[chunk, plane], root.at[chunk, plane], chunk, MEAN)

    def clipped(chunk):
        wait_for(root.at[chunk, pl.ds(0, PLANES - 1)], recv_sem.at[MEAN, chunk])
        here, opposite = bound[0, chunk] * root[chunk], bound[1, chunk] * root[chunk]
        real, imag = spec[chunk, :, :, :LANES], spec[chunk, :, :, LANES:]
        return [
            0.5 * (jnp.clip(value, -here, here) + jnp.clip(value, -opposite, opposite)) for value in (real, imag)
        ]

    def backward(chunk):
        real, imag = clipped(chunk)
        sym[:, :, :LANES] = real
        sym[:, :, LANES:] = imag
        if chunk == 0:

            @pl.when(special)
            def _():
                real, imag = clipped(SPECIAL)
                place = (row == 0)[None] & (lane < HALF)[None]
                sym[:, :, :LANES] = jnp.where(place, real - pltpu.roll(imag, HALF, 2), sym[:, :, :LANES])
                sym[:, :, LANES:] = jnp.where(place, imag + pltpu.roll(real, HALF, 2), sym[:, :, LANES:])

        back[chunk] = x_inverse(sym[...], (xi[0], xi[1]), xt)
        all_to_all(back, returned, chunk, BACK)

    def along_y(chunk):
        wait_for(returned.at[chunk], recv_sem.at[BACK, chunk])
        for index in (2 * chunk, 2 * chunk + 1):
            first = 16 * (index % 2)
            rows = returned[chunk, first : first + 16].reshape(LANES, LANES)
            width = 2 * LANES if index else 3 * LANES
            total = product(split(rows), (yi[0, :, :width], yi[1, :, :width]), ((0,), (0,)))
            lines[index, 0], lines[index, 1] = y_line(total, index, yt[0], yt[1])

    forward(0)

    @pl.when(special)
    def _():
        blocks = received[0]
        turned = pltpu.roll(pltpu.roll(blocks, HALF, 2), 4, 1)
        blocks = jnp.where((lane < HALF)[None], blocks, turned)
        along_x(jnp.where(upper(blocks.shape), blocks, 0.0), SPECIAL)

    forward(1)
    average(0)

    @pl.when(special)
    def _():
        average(SPECIAL)

    forward(2)
    average(1)
    forward(3)
    backward(0)
    average(2)
    backward(1)
    average(3)
    backward(2)
    backward(3)

    for chunk in range(CHUNKS):
        along_y(chunk)
    for index, value in enumerate(y_result([(lines[index, 0], lines[index, 1]) for index in range(8)])):
        out[:, index, :] = value

    for chunk in range(CHUNKS):
        for kind in (SEND, BACK):
            wait_for(received.at[chunk], send_sem.at[kind, chunk])
        for kind in (POWER, MEAN):
            wait_for(powers.at[chunk, pl.ds(0, PLANES - 1)], send_sem.at[kind, chunk])

    @pl.when(special)
    def _():
        for kind in (POWER, MEAN):
            wait_for(powers.at[SPECIAL, pl.ds(0, PLANES - 1)], send_sem.at[kind, SPECIAL])


def correct(error_field, x_shape, y_shape):
    shape = (OWN, 16, LANES)
    operands = [
        error_field.reshape(shape), y_forward_table(), y_inverse_table(), x_table(-1), x_table(1), y_twist(), x_twist(), *x_choices(),
        x_shape.reshape(16, LANES), y_shape,
    ]
    operands = [jnp.asarray(operand) for operand in operands]
    inside = [pltpu.VMEM(operand.shape, operand.dtype) for operand in operands]
    inside[-1] = pltpu.SMEM(y_shape.shape, F32)
    outside = pl.BlockSpec(memory_space=pltpu.HBM)
    done = pl.pallas_call(
        kernel,
        out_shape=pltpu.VMEM(shape, F32),
        in_specs=[outside] * len(operands),
        out_specs=pl.BlockSpec(memory_space=pltpu.VMEM),
        scratch_shapes=inside
        + [
            pltpu.VMEM((CHUNKS, FFT, 8, LANES), F32),
            pltpu.VMEM((CHUNKS, FFT, 8, LANES), F32),
            pltpu.VMEM((CHUNKS + 1, 16, 8, 2 * LANES), F32),
            pltpu.VMEM((CHUNKS + 1, PLANES, 8, LANES), F32),
            pltpu.VMEM((CHUNKS + 1, PLANES, 8, LANES), F32),
            pltpu.VMEM((CHUNKS + 1, PLANES, 8, LANES), F32),
            pltpu.VMEM((2, CHUNKS + 1, 16, 8, LANES), F32),
            pltpu.VMEM((CHUNKS, FFT, 8, LANES), F32),
            pltpu.VMEM((CHUNKS, FFT, 8, LANES), F32),
            pltpu.VMEM((16, 8, 2 * LANES), F32),
            pltpu.VMEM((8, 2, OWN, LANES), F32),
            pltpu.SemaphoreType.DMA((len(operands),)),
            pltpu.SemaphoreType.DMA((4, CHUNKS + 1)),
            pltpu.SemaphoreType.DMA((4, CHUNKS + 1)),
        ],
        compiler_params=pltpu.CompilerParams(
            collective_id=0, has_side_effects=True, vmem_limit_bytes=60 * 1024 * 1024
        ),
    )(*operands)
    return done.reshape(error_field.shape)


def solution(mesh):
    placed = (P("fft", "plane", None), P(), P())
    return jax.shard_map(
        correct, mesh=mesh, in_specs=placed, out_specs=P("fft", "plane", None), check_vma=False
    )
```
